512 devices in a mesh: freq: 8 (over y_hi, core), row: 64 (over z, y_lo, x).
Axes of the slice: x: 4, y: 8 (y_hi: 4, y_lo: 2; y = y_hi * 2 + y_lo), z: 8, core: 2. Of those that a mesh axis runs over, the one named last changes fastest.
Arguments:
- field: float32 [2, 8, 2048, 2048], P(None, 'freq', 'row'), may hold values from -6 to 6
- layer_index: int32 [2048], replicated, may hold values from 0 to 15
- layer_slowness: float32 [16], replicated, may hold values from 0.2223 to 0.6666
Outputs:
- sunk_field: float32 [2, 8, 2048, 2048], P(None, 'freq', None, 'row')
- image: float32 [128, 2048], P(None, 'row')
The draws below stay inside these ranges and needn't reach their ends.
All inputs are finite; a program needn't handle non-finite values.
Results may differ from the reference program's by a relative error of at most 0.000078.
Values sent between devices are 32-bit elements; how exact they have to be, the bound alone decides.
No kernel may reach another device: no remote copies, remote signals or barrier semaphores. Data moves between devices by JAX's collectives and lax.ppermute only.
A program may use at most 64 MiB of HBM per device.

```python
import math
import jax
import jax.numpy as jnp
from jax import lax

NX = 2048
NL = 16
HOFF = 128
NF = 8


def plant(result, own_key, least, largest):
    dims = result.shape
    spot = [jax.random.randint(jax.random.fold_in(own_key, axis), (), 0, dims[axis]) for axis in range(len(dims))]
    result = result.at[tuple(spot)].set(least)
    longest = dims.index(max(dims))
    spot[longest] = (spot[longest] + 1) % dims[longest]
    return result.at[tuple(spot)].set(largest)


def steps_of(stream_key, dims, cuts, least, largest):
    gain, own = 1.0, jax.random.fold_in(stream_key, 6)
    for dim, parts in cuts:
        draws = jnp.exp(jax.random.uniform(jax.random.fold_in(own, dim), (parts,), jnp.float32, least / len(cuts), largest / len(cuts)))
        gain = gain * jnp.repeat(draws, dims[dim] // parts).reshape([-1 if axis == dim else 1 for axis in range(len(dims))])
    return gain


def noise(stream_key, shape, deviation, most, shards=(), kind=jnp.bfloat16):
    result = deviation * jax.random.normal(stream_key, shape, jnp.float32)
    if shards:
        result = result * steps_of(stream_key, shape, shards, -0.22, 0.18)
    return jnp.clip(result, -most, most).astype(kind)


def setup_inputs(seed: int = 0) -> dict:
    arg_keys = jax.random.split(jax.random.key(seed), 4)
    field = noise(arg_keys[0], (2, NF, NX, NX), 1.0, 6.0, ((1, 8), (2, 64)), jnp.float32)
    layer_index = plant(jax.random.randint(arg_keys[1], (NX,), 0, NL), jax.random.fold_in(arg_keys[1], 1), 0, NL - 1).astype(jnp.int32)
    layer_slowness = jnp.clip(jnp.exp(jax.random.uniform(arg_keys[2], (NL,), jnp.float32, math.log(0.2223), math.log(0.6666))), 0.2223, 0.6666)
    return dict(field=field, layer_index=layer_index, layer_slowness=layer_slowness)


depth_step = 0.0125
grid_step = 0.0125
slow_slow = 1.0 / 1.5
slow_fast = 1.0 / 4.5

def wavenumbers(count):
    index = jnp.arange(count, dtype=jnp.int32)
    signed = jnp.where(index < count // 2, index, index - count)
    return signed.astype(jnp.float32) * (2.0 * math.pi / (count * grid_step))

def reference(field, layer_index, layer_slowness):
    total = field.shape[1]
    onehot = (layer_index[None, :] == jnp.arange(NL, dtype=jnp.int32)[:, None]).astype(jnp.float32)
    slowness = lax.optimization_barrier(jnp.sum(layer_slowness[:, None] * onehot, axis=0))
    upper = (slow_slow - slowness) / (slow_slow - slow_fast)
    lower = 1.0 - upper
    weights = (lower, upper)
    refs = (slow_slow, slow_fast)
    knum = wavenumbers(NX)
    fidx = jnp.arange(total, dtype=jnp.int32).astype(jnp.float32)
    omegas = 2.0 * math.pi * (5.0 + 30.0 * (fidx + 0.5) / total)
    shot_at = (jnp.arange(NX, dtype=jnp.int32)[None, :] + jnp.arange(HOFF, dtype=jnp.int32)[:, None] - HOFF // 2) % NX

    def tables(omega):
        props, corrs = ([], [])
        for j in range(2):
            quad = (omega * refs[j]) ** 2 - knum * knum
            mag = jnp.exp(-depth_step * jnp.sqrt(jnp.maximum(-quad, 0.0)))
            phase = -depth_step * jnp.sqrt(jnp.maximum(quad, 0.0))
            props.append(mag * jnp.cos(phase) + 1j * (mag * jnp.sin(phase)))
            angle = -omega * depth_step * (slowness - refs[j])
            corrs.append(weights[j] * jnp.cos(angle) + 1j * (weights[j] * jnp.sin(angle)))
        return (props, corrs)

    def one(items):
        real, imag, omega = items
        props, corrs = tables(omega)
        wave = real + 1j * imag
        spec = jnp.fft.fft(wave, axis=1)
        sunk = corrs[0][None, :] * jnp.fft.ifft(spec * props[0][None, :], axis=1)
        sunk = sunk + corrs[1][None, :] * jnp.fft.ifft(spec * props[1][None, :], axis=1)
        spec = jnp.fft.fft(sunk, axis=0)
        out = corrs[0][:, None] * jnp.fft.ifft(spec * props[0][:, None], axis=0)
        out = out + corrs[1][:, None] * jnp.fft.ifft(spec * props[1][:, None], axis=0)
        out_re = jnp.real(out)
        out_im = jnp.imag(out)
        picked = jnp.take_along_axis(out_re, shot_at, axis=0)
        return (out_re, out_im, picked)
    out_re, out_im, picked = lax.map(one, (field[0], field[1], omegas))
    return (jnp.stack([out_re, out_im]), lax.optimization_barrier(jnp.sum(picked, axis=0)))
```

```python
import math

import jax
import jax.numpy as jnp
import ml_dtypes
import numpy as np
from jax import lax
from jax.experimental import pallas as pl
from jax.experimental.pallas import tpu as pltpu
from jax.sharding import PartitionSpec as P

HOFF = 128
NX = 2048
NL = 16
BLOCK = 32
HIGH = 16
LANES = 128

depth_step = 0.0125
grid_step = 0.0125
slow_slow = 1.0 / 1.5
slow_fast = 1.0 / 4.5
refs = (slow_slow, slow_fast)


def split16(table):
    high = table.astype(np.float32).astype(ml_dtypes.bfloat16)
    low = (table - high.astype(np.float64)).astype(np.float32).astype(ml_dtypes.bfloat16)
    return high, low


def dft_weights():
    lane = np.arange(LANES)
    angle = 2.0 * math.pi * (lane[:, None] * lane[None, :] % LANES) / LANES
    cos, sin = np.cos(angle), np.sin(angle)
    forward = np.block([[cos, -sin], [sin, cos]])
    inverse = np.block([[cos, sin], [-sin, cos]])
    return np.stack(split16(forward) + split16(inverse))


def twiddle_table():
    angle = 2.0 * math.pi * np.arange(HIGH)[:, None] * np.arange(LANES)[None, :] / NX
    return np.stack([np.cos(angle), -np.sin(angle)]).astype(np.float32)


def omega_of(index, total):
    return 2.0 * math.pi * (5.0 + 30.0 * (index + 0.5) / total)


def propagators(total):
    index = np.arange(NX)
    knum = np.where(index < NX // 2, index, index - NX) * (2.0 * math.pi / (NX * grid_step))
    out = np.zeros((total, 2, 2, HIGH, LANES), np.float32)
    for f in range(total):
        for j in range(2):
            quad = (omega_of(f, total) * refs[j]) ** 2 - knum**2
            mag = np.exp(-depth_step * np.sqrt(np.maximum(-quad, 0.0)))
            phase = -depth_step * np.sqrt(np.maximum(quad, 0.0))
            out[f, j, 0] = (mag * np.cos(phase)).reshape(LANES, HIGH).T
            out[f, j, 1] = (mag * np.sin(phase)).reshape(LANES, HIGH).T
    return out


def add(a, b):
    return a[0] + b[0], a[1] + b[1]


def sub(a, b):
    return a[0] - b[0], a[1] - b[1]


def mul(a, b):
    return a[0] * b[0] - a[1] * b[1], a[0] * b[1] + a[1] * b[0]


def mul_conj(a, b):
    return a[0] * b[0] + a[1] * b[1], a[1] * b[0] - a[0] * b[1]


def fft4(x, sign):
    t0, t1 = add(x[0], x[2]), sub(x[0], x[2])
    t2, t3 = add(x[1], x[3]), sub(x[1], x[3])
    up = (t1[0] - t3[1], t1[1] + t3[0])
    down = (t1[0] + t3[1], t1[1] - t3[0])
    if sign < 0:
        up, down = down, up
    return [add(t0, t2), up, sub(t0, t2), down]


def turn(x, step, sign):
    step = step % 16
    if step == 0:
        return x
    if step == 4:
        return (x[1], -x[0]) if sign < 0 else (-x[1], x[0])
    root = math.sqrt(0.5)
    if step == 2:
        if sign < 0:
            return (x[0] + x[1]) * root, (x[1] - x[0]) * root
        return (x[0] - x[1]) * root, (x[1] + x[0]) * root
    angle = sign * 2.0 * math.pi * step / 16
    return mul(x, (math.cos(angle), math.sin(angle)))


def fft16(x, sign):
    parts = [fft4([x[4 * m + n] for m in range(4)], sign) for n in range(4)]
    out = [None] * 16
    for k in range(4):
        col = fft4([turn(parts[n][k], n * k, sign) for n in range(4)], sign)
        for m in range(4):
            out[k + 4 * m] = col[m]
    return out


def halves(x):
    high = x.astype(jnp.bfloat16)
    return high, (x - high.astype(jnp.float32)).astype(jnp.bfloat16)


def dot3(high, low, w_high, w_low):
    dot = lambda a, b: jnp.dot(a, b, preferred_element_type=jnp.float32)
    return dot(high, w_high) + dot(low, w_high) + dot(high, w_low)


def sink(x, w_ref, tw_ref, e_ref, corr):
    rows = x[0][0].shape[0]
    row = lambda ref, i: ref[pl.ds(i, 1), :]
    y = fft16(x, -1)
    y = [mul(y[k], (row(tw_ref.at[0], k), row(tw_ref.at[1], k))) for k in range(HIGH)]
    flat = jnp.concatenate([jnp.concatenate(v, axis=1) for v in y], axis=0)
    spec = dot3(*halves(flat), w_ref[0], w_ref[1])
    result = [None] * HIGH
    for j in range(2):
        moved = []
        for k in range(HIGH):
            part = spec[k * rows : (k + 1) * rows]
            e = (row(e_ref.at[0, j, 0], k), row(e_ref.at[0, j, 1], k))
            moved.append(jnp.concatenate(mul((part[:, :LANES], part[:, LANES:]), e), axis=1))
        back = dot3(*halves(jnp.concatenate(moved, axis=0)), w_ref[2], w_ref[3])
        v = []
        for k in range(HIGH):
            part = back[k * rows : (k + 1) * rows]
            v.append(
                mul_conj(
                    (part[:, :LANES], part[:, LANES:]), (row(tw_ref.at[0], k), row(tw_ref.at[1], k))
                )
            )
        v = fft16(v, 1)
        for a in range(HIGH):
            term = mul(v[a], corr(j, a))
            result[a] = term if j == 0 else add(result[a], term)
    return result


def fill_corrections(index_ref, slow_ref, omega, corr_ref):
    index = index_ref[...]
    slowness = jnp.zeros(index.shape, jnp.float32)
    for layer in range(NL):
        slowness = jnp.where(index == layer, slow_ref[layer], slowness)
    upper = (slow_slow - slowness) / (slow_slow - slow_fast)
    weights = (1.0 - upper, upper)
    for j in range(2):
        angle = -omega * depth_step * (slowness - refs[j])
        corr_ref[j, 0] = weights[j] * jnp.cos(angle) * (1.0 / NX)
        corr_ref[j, 1] = weights[j] * jnp.sin(angle) * (1.0 / NX)


def corr_rows(corr_ref):
    def get(j, a):
        return corr_ref[j, 0, pl.ds(a, 1), :], corr_ref[j, 1, pl.ds(a, 1), :]

    return get


def first_kernel(total, freq_ref, slow_ref, field_ref, index_ref, w_ref, tw_ref, e_ref, out_ref, corr_ref, sunk):
    omega = 2.0 * math.pi * (5.0 + 30.0 * (freq_ref[0].astype(jnp.float32) + 0.5) / total)
    fill_corrections(index_ref, slow_ref, omega, corr_ref)

    def rows16(h, _):
        at = pl.ds(pl.multiple_of(h * 16, 16), 16)
        x = [
            (field_ref[0, at, LANES * a : LANES * (a + 1)], field_ref[1, at, LANES * a : LANES * (a + 1)])
            for a in range(HIGH)
        ]
        u = sink(x, w_ref, tw_ref, e_ref, corr_rows(corr_ref))
        for a in range(HIGH):
            for c in range(2):
                base = (a % 2) * 64 + c * 32
                sunk[a // 2, pl.ds(pl.multiple_of(base + h * 16, 16), 16), :] = u[a][c]
        return 0

    lax.fori_loop(0, 2, rows16, 0)
    left = lax.broadcasted_iota(jnp.int32, (16, LANES), 1) < 64

    def pair(p, _):
        turned = sunk[p].T
        for q in range(4):
            upper = turned[32 * q : 32 * q + 16]
            lower = turned[32 * q + 16 : 32 * q + 32]
            first = jnp.where(left, upper, pltpu.roll(lower, 64, 1))
            second = jnp.where(left, pltpu.roll(upper, 64, 1), lower)
            out_ref[pl.ds(pl.multiple_of(p * 128 + 16 * q, 16), 16), :] = first
            out_ref[pl.ds(pl.multiple_of(p * 128 + 64 + 16 * q, 16), 16), :] = second
        return 0

    lax.fori_loop(0, HIGH // 2, pair, 0)


def second_kernel(freq_ref, block_ref, in_ref, corr_ref, w_ref, tw_ref, e_ref, out_ref, image_ref, lined):
    lane = lax.broadcasted_iota(jnp.int32, (16, LANES), 1)
    left = lane < 64
    even = lane % 64 < 32

    def regroup(a, _):
        g = [in_ref[pl.ds(pl.multiple_of(a * 64 + 16 * q, 16), 16), :] for q in range(4)]

        def swap(x, y, mask, width):
            return (
                jnp.where(mask, x, pltpu.roll(y, width, 1)),
                jnp.where(mask, pltpu.roll(x, LANES - width, 1), y),
            )

        p0, p2 = swap(g[0], g[2], left, 64)
        p1, p3 = swap(g[1], g[3], left, 64)
        o0, o1 = swap(p0, p1, even, 32)
        o2, o3 = swap(p2, p3, even, 32)
        lined[0, 0, a] = o0
        lined[0, 1, a] = o1
        lined[1, 0, a] = o2
        lined[1, 1, a] = o3
        return 0

    lax.fori_loop(0, HIGH, regroup, 0)

    def rows16(h, _):
        x = [(lined[h, 0, a], lined[h, 1, a]) for a in range(HIGH)]
        u = sink(x, w_ref, tw_ref, e_ref, corr_rows(corr_ref))
        at = pl.ds(pl.multiple_of(h * 16, 16), 16)
        for a in range(HIGH):
            for c in range(2):
                out_ref[c, at, LANES * a : LANES * (a + 1)] = u[a][c]
        return 0

    lax.fori_loop(0, 2, rows16, 0)
    start = (block_ref[0] * BLOCK + NX - HOFF // 2) % NX
    tile = start // LANES
    offset = start % LANES
    one = out_ref[0, :, pl.ds(pl.multiple_of(tile * LANES, LANES), LANES)]
    two = out_ref[0, :, pl.ds(pl.multiple_of((tile + 1) % HIGH * LANES, LANES), LANES)]
    band = jnp.concatenate([one, two], axis=1)
    row = lax.broadcasted_iota(jnp.int32, (BLOCK, 2 * LANES), 0) + offset
    for bit in range(7):
        step = 1 << bit
        band = jnp.where((row // step) % 2 == 1, pltpu.roll(band, 2 * LANES - step, 1), band)
    image_ref[...] = band[:, :LANES]


def on_device(field, layer_index, layer_slowness):
    total = lax.axis_size("freq")
    groups = lax.axis_size("row")
    weights = jnp.asarray(dft_weights())
    twiddles = jnp.asarray(twiddle_table())
    props = jnp.asarray(propagators(total))
    freq = lax.axis_index("freq").astype(jnp.int32).reshape(1)
    row = lax.axis_index("row").astype(jnp.int32).reshape(1)
    whole = lambda *shape: pl.BlockSpec(shape, lambda i, *_: (0,) * len(shape))
    mine = pl.BlockSpec((1, 2, 2, HIGH, LANES), lambda i, f, *_: (f[0], 0, 0, 0, 0))
    tables = [whole(4, 256, 256), whole(2, HIGH, LANES), mine]
    chunks, corr = pl.pallas_call(
        lambda *a: first_kernel(total, *a),
        out_shape=(
            jax.ShapeDtypeStruct((16 * groups, LANES), jnp.float32),
            jax.ShapeDtypeStruct((2, 2, HIGH, LANES), jnp.float32),
        ),
        grid_spec=pltpu.PrefetchScalarGridSpec(
            num_scalar_prefetch=2,
            grid=(1,),
            in_specs=[whole(2, BLOCK, NX), whole(HIGH, LANES)] + tables,
            out_specs=(whole(16 * groups, LANES), whole(2, 2, HIGH, LANES)),
            scratch_shapes=[pltpu.VMEM((HIGH // 2, LANES, LANES), jnp.float32)],
        ),
        compiler_params=pltpu.CompilerParams(vmem_limit_bytes=32 * 2**20),
        name="receiver_side",
    )(
        freq,
        layer_slowness,
        field.reshape(2, BLOCK, NX),
        layer_index.reshape(HIGH, LANES),
        weights,
        twiddles,
        props,
    )
    arrived = lax.all_to_all(chunks.reshape(groups, 1, NX), "row", 0, 0, tiled=True)
    sunk, image = pl.pallas_call(
        second_kernel,
        out_shape=(
            jax.ShapeDtypeStruct((2, BLOCK, NX), jnp.float32),
            jax.ShapeDtypeStruct((BLOCK, HOFF), jnp.float32),
        ),
        grid_spec=pltpu.PrefetchScalarGridSpec(
            num_scalar_prefetch=2,
            grid=(1,),
            in_specs=[whole(16 * groups, LANES), whole(2, 2, HIGH, LANES)] + tables,
            out_specs=(whole(2, BLOCK, NX), whole(BLOCK, HOFF)),
            scratch_shapes=[pltpu.VMEM((2, 2, HIGH, 16, LANES), jnp.float32)],
        ),
        compiler_params=pltpu.CompilerParams(vmem_limit_bytes=32 * 2**20),
        name="shot_side",
    )(freq, row, arrived.reshape(16 * groups, LANES), corr, weights, twiddles, props)
    image = jnp.swapaxes(lax.psum(image, "freq"), 0, 1)
    return jnp.swapaxes(sunk, 1, 2)[:, None], image


def solution(mesh):
    return jax.shard_map(
        on_device,
        mesh=mesh,
        in_specs=(P(None, "freq", "row", None), P(), P()),
        out_specs=(P(None, "freq", None, "row"), P(None, "row")),
        check_vma=False,
    )
```

```python
import math

import jax
import jax.numpy as jnp
import ml_dtypes
import numpy as np
from jax import lax
from jax.experimental import pallas as pl
from jax.experimental.pallas import tpu as pltpu
from jax.sharding import PartitionSpec as P

HOFF = 128
NX = 2048
NL = 16
BLOCK = 32
HIGH = 16
LANES = 128

depth_step = 0.0125
grid_step = 0.0125
slow_slow = 1.0 / 1.5
slow_fast = 1.0 / 4.5
refs = (slow_slow, slow_fast)


def split16(table):
    high = table.astype(np.float32).astype(ml_dtypes.bfloat16)
    low = (table - high.astype(np.float64)).astype(np.float32).astype(ml_dtypes.bfloat16)
    return high, low


def dft_weights():
    lane = np.arange(LANES)
    angle = 2.0 * math.pi * (lane[:, None] * lane[None, :] % LANES) / LANES
    cos, sin = np.cos(angle), np.sin(angle)
    forward = np.block([[cos, -sin], [sin, cos]])
    inverse = np.block([[cos, sin], [-sin, cos]])
    return np.stack(split16(forward) + split16(inverse))


def twiddle_table():
    angle = 2.0 * math.pi * np.arange(HIGH)[:, None] * np.arange(LANES)[None, :] / NX
    return np.stack([np.cos(angle), -np.sin(angle)]).astype(np.float32)


def omega_of(index, total):
    return 2.0 * math.pi * (5.0 + 30.0 * (index + 0.5) / total)


def propagators(total):
    index = np.arange(NX)
    knum = np.where(index < NX // 2, index, index - NX) * (2.0 * math.pi / (NX * grid_step))
    out = np.zeros((total, 2, 2, HIGH, LANES), np.float32)
    for f in range(total):
        for j in range(2):
            quad = (omega_of(f, total) * refs[j]) ** 2 - knum**2
            mag = np.exp(-depth_step * np.sqrt(np.maximum(-quad, 0.0)))
            phase = -depth_step * np.sqrt(np.maximum(quad, 0.0))
            out[f, j, 0] = (mag * np.cos(phase)).reshape(LANES, HIGH).T
            out[f, j, 1] = (mag * np.sin(phase)).reshape(LANES, HIGH).T
    return out


def add(a, b):
    return a[0] + b[0], a[1] + b[1]


def sub(a, b):
    return a[0] - b[0], a[1] - b[1]


def mul(a, b):
    return a[0] * b[0] - a[1] * b[1], a[0] * b[1] + a[1] * b[0]


def mul_conj(a, b):
    return a[0] * b[0] + a[1] * b[1], a[1] * b[0] - a[0] * b[1]


def fft4(x, sign):
    t0, t1 = add(x[0], x[2]), sub(x[0], x[2])
    t2, t3 = add(x[1], x[3]), sub(x[1], x[3])
    up = (t1[0] - t3[1], t1[1] + t3[0])
    down = (t1[0] + t3[1], t1[1] - t3[0])
    if sign < 0:
        up, down = down, up
    return [add(t0, t2), up, sub(t0, t2), down]


def turn(x, step, sign):
    step = step % 16
    if step == 0:
        return x
    if step == 4:
        return (x[1], -x[0]) if sign < 0 else (-x[1], x[0])
    root = math.sqrt(0.5)
    if step == 2:
        if sign < 0:
            return (x[0] + x[1]) * root, (x[1] - x[0]) * root
        return (x[0] - x[1]) * root, (x[1] + x[0]) * root
    angle = sign * 2.0 * math.pi * step / 16
    return mul(x, (math.cos(angle), math.sin(angle)))


def fft16(x, sign):
    parts = [fft4([x[4 * m + n] for m in range(4)], sign) for n in range(4)]
    out = [None] * 16
    for k in range(4):
        col = fft4([turn(parts[n][k], n * k, sign) for n in range(4)], sign)
        for m in range(4):
            out[k + 4 * m] = col[m]
    return out


def halves(x):
    high = x.astype(jnp.bfloat16)
    return high, (x - high.astype(jnp.float32)).astype(jnp.bfloat16)


def dot3(high, low, w_high, w_low):
    dot = lambda a, b: jnp.dot(a, b, preferred_element_type=jnp.float32)
    return dot(high, w_high) + dot(low, w_high) + dot(high, w_low)


def row(ref, i):
    return ref[pl.ds(i, 1), :]


def spread(x, w_ref, tw_ref, e_ref):
    rows = x[0][0].shape[0]
    twiddle = lambda k: (row(tw_ref.at[0], k), row(tw_ref.at[1], k))
    y = fft16(x, -1)
    flat = jnp.concatenate(
        [jnp.concatenate(mul(y[k], twiddle(k)), axis=1) for k in range(HIGH)], axis=0
    )
    spec = dot3(*halves(flat), w_ref[0], w_ref[1])
    for j in range(2):
        moved = []
        for k in range(HIGH):
            part = spec[k * rows : (k + 1) * rows]
            e = (row(e_ref.at[0, j, 0], k), row(e_ref.at[0, j, 1], k))
            moved.append(jnp.concatenate(mul((part[:, :LANES], part[:, LANES:]), e), axis=1))
        back = dot3(*halves(jnp.concatenate(moved, axis=0)), w_ref[2], w_ref[3])
        tiles = []
        for k in range(HIGH):
            part = back[k * rows : (k + 1) * rows]
            tiles.append(mul_conj((part[:, :LANES], part[:, LANES:]), twiddle(k)))
        yield j, tiles


def corr_row(corr_ref, j, a):
    return row(corr_ref.at[j, 0], a), row(corr_ref.at[j, 1], a)


def gather_up(corr_ref, tiles_of):
    result = [None] * HIGH
    for j, tiles in tiles_of:
        v = fft16(tiles, 1)
        for a in range(HIGH):
            term = mul(v[a], corr_row(corr_ref, j, a))
            result[a] = term if j == 0 else add(result[a], term)
    return result


def fill_corrections(index_ref, slow_ref, omega, corr_ref):
    index = index_ref[...]
    slowness = jnp.zeros(index.shape, jnp.float32)
    for layer in range(NL):
        slowness = jnp.where(index == layer, slow_ref[layer], slowness)
    upper = (slow_slow - slowness) / (slow_slow - slow_fast)
    weights = (1.0 - upper, upper)
    for j in range(2):
        angle = -omega * depth_step * (slowness - refs[j])
        corr_ref[j, 0] = weights[j] * jnp.cos(angle) * (1.0 / NX)
        corr_ref[j, 1] = weights[j] * jnp.sin(angle) * (1.0 / NX)


def first_kernel(
    total, slow_hbm, index_hbm, field_hbm, tw_hbm, w_hbm, e_hbm, out_ref, corr_ref,
    slow_ref, index_ref, field_ref, tw_ref, w_ref, e_ref, sunk, sems,
):
    freq = lax.axis_index("freq")
    pairs = [
        (slow_hbm, slow_ref),
        (index_hbm, index_ref),
        (field_hbm, field_ref),
        (tw_hbm, tw_ref),
        (w_hbm, w_ref),
        (e_hbm.at[pl.ds(freq, 1)], e_ref),
    ]
    copies = [pltpu.make_async_copy(s, d, sems.at[i]) for i, (s, d) in enumerate(pairs)]
    for copy in copies:
        copy.start()
    copies[0].wait()
    copies[1].wait()
    omega = 2.0 * math.pi * (5.0 + 30.0 * (freq.astype(jnp.float32) + 0.5) / total)
    fill_corrections(index_ref, slow_ref, omega, corr_ref)
    for copy in copies[2:]:
        copy.wait()

    def rows16(h, _):
        at = pl.ds(pl.multiple_of(h * 16, 16), 16)
        x = [
            (field_ref[0, at, LANES * a : LANES * (a + 1)], field_ref[1, at, LANES * a : LANES * (a + 1)])
            for a in range(HIGH)
        ]
        u = gather_up(corr_ref, spread(x, w_ref, tw_ref, e_ref))
        for a in range(HIGH):
            for c in range(2):
                base = (a % 2) * 64 + c * 32
                sunk[a // 2, pl.ds(pl.multiple_of(base + h * 16, 16), 16), :] = u[a][c]
        return 0

    lax.fori_loop(0, 2, rows16, 0)
    left = lax.broadcasted_iota(jnp.int32, (16, LANES), 1) < 64
    for p in range(HIGH // 2):
        turned = sunk[p].T
        for q in range(4):
            upper = turned[32 * q : 32 * q + 16]
            lower = turned[32 * q + 16 : 32 * q + 32]
            first = jnp.where(left, upper, pltpu.roll(lower, 64, 1))
            second = jnp.where(left, pltpu.roll(upper, 64, 1), lower)
            out_ref[p * 128 + 16 * q : p * 128 + 16 * q + 16, :] = first
            out_ref[p * 128 + 64 + 16 * q : p * 128 + 80 + 16 * q, :] = second


def second_kernel(root_ref, in_ref, corr_ref, w_ref, tw_ref, e_all, parts_ref, image_hbm, lined, image_ref, sems):
    lane = lax.broadcasted_iota(jnp.int32, (16, LANES), 1)
    left = lane < 64
    even = (lane & 63) < 32
    e_ref = e_all.at[pl.ds(lax.axis_index("freq"), 1)]

    def swap(x, y, mask, width):
        return (
            jnp.where(mask, x, pltpu.roll(y, width, 1)),
            jnp.where(mask, pltpu.roll(x, LANES - width, 1), y),
        )

    for a in range(HIGH):
        g = [in_ref[a * 64 + 16 * q : a * 64 + 16 * q + 16, :] for q in range(4)]
        p0, p2 = swap(g[0], g[2], left, 64)
        p1, p3 = swap(g[1], g[3], left, 64)
        lined[0, 0, a], lined[0, 1, a] = swap(p0, p1, even, 32)
        lined[1, 0, a], lined[1, 1, a] = swap(p2, p3, even, 32)

    start = (lax.axis_index("row") * BLOCK + NX - HOFF // 2) & (NX - 1)
    tile = start // LANES
    offset = start & (LANES - 1)

    def rows16(h, _):
        x = [(lined[h, 0, a], lined[h, 1, a]) for a in range(HIGH)]
        at = pl.ds(pl.multiple_of(h * 16, 16), 16)
        band = [0.0, 0.0]
        for j, tiles in spread(x, w_ref, tw_ref, e_ref):
            for k in range(HIGH):
                parts_ref[j, 0, k, at, :] = tiles[k][0]
                parts_ref[j, 1, k, at, :] = tiles[k][1]
            for i in range(2):
                a = (tile + i) & (HIGH - 1)
                here = None
                for k in range(HIGH):
                    turned = mul(tiles[k], (root_ref[0, (a * k) & 15], root_ref[1, (a * k) & 15]))
                    here = turned if here is None else add(here, turned)
                c = corr_row(corr_ref, j, a)
                band[i] = band[i] + here[0] * c[0] - here[1] * c[1]
        image_ref[at, :] = jnp.concatenate(band, axis=1)
        return 0

    lax.fori_loop(0, 2, rows16, 0)
    band = image_ref[...]
    for width in (64, 32):
        band = jnp.where((offset & width) != 0, pltpu.roll(band, 2 * LANES - width, 1), band)
    line = lax.broadcasted_iota(jnp.int32, band.shape, 0)
    for width in (16, 8, 4, 2, 1):
        band = jnp.where((line & width) != 0, pltpu.roll(band, 2 * LANES - width, 1), band)
    image_ref[:, :LANES] = band[:, :LANES]
    copies = [
        pltpu.make_async_copy(image_ref.at[:, pl.ds(0, LANES)], image_hbm.at[f], sems.at[f])
        for f in range(image_hbm.shape[0])
    ]
    for copy in copies:
        copy.start()
    for copy in copies:
        copy.wait()


def third_kernel(parts_ref, corr_ref, out_ref):
    def rows16(h, _):
        at = pl.ds(pl.multiple_of(h * 16, 16), 16)
        tiles_of = [
            (j, [(parts_ref[j, 0, k, at, :], parts_ref[j, 1, k, at, :]) for k in range(HIGH)])
            for j in range(2)
        ]
        u = gather_up(corr_ref, tiles_of)
        for a in range(HIGH):
            for c in range(2):
                out_ref[c, at, LANES * a : LANES * (a + 1)] = u[a][c]
        return 0

    lax.fori_loop(0, 2, rows16, 0)


def on_device(field, layer_index, layer_slowness):
    total = lax.axis_size("freq")
    groups = lax.axis_size("row")
    weights = jnp.asarray(dft_weights())
    twiddles = jnp.asarray(twiddle_table())
    props = jnp.asarray(propagators(total))
    angle = 2.0 * math.pi * np.arange(16) / 16
    roots = jnp.asarray(np.stack([np.cos(angle), np.sin(angle)]).astype(np.float32))
    shape = lambda *dims: jax.ShapeDtypeStruct(dims, jnp.float32)
    keep = lambda *dims: pltpu.VMEM(dims, jnp.float32)
    vmem = pl.BlockSpec(memory_space=pltpu.VMEM)
    smem = pl.BlockSpec(memory_space=pltpu.SMEM)
    hbm = pl.BlockSpec(memory_space=pltpu.HBM)
    stay = lambda x: pltpu.with_memory_space_constraint(x, pltpu.HBM)
    near = lambda x: pltpu.with_memory_space_constraint(x, pltpu.VMEM)
    params = pltpu.CompilerParams(vmem_limit_bytes=32 * 2**20)
    cost = lambda n: pl.CostEstimate(flops=n, bytes_accessed=2**20, transcendentals=0)
    chunks, corr = pl.pallas_call(
        lambda *a: first_kernel(total, *a),
        out_shape=(keep(16 * groups, LANES), keep(2, 2, HIGH, LANES)),
        in_specs=[hbm] * 6,
        out_specs=(vmem, vmem),
        scratch_shapes=[
            pltpu.SMEM((NL,), jnp.float32),
            pltpu.VMEM((HIGH, LANES), jnp.int32),
            pltpu.VMEM((2, BLOCK, NX), jnp.float32),
            pltpu.VMEM((2, HIGH, LANES), jnp.float32),
            pltpu.VMEM((4, 256, 256), jnp.bfloat16),
            pltpu.VMEM((1, 2, 2, HIGH, LANES), jnp.float32),
            pltpu.VMEM((HIGH // 2, LANES, LANES), jnp.float32),
            pltpu.SemaphoreType.DMA((6,)),
        ],
        compiler_params=params,
        cost_estimate=cost(10**9),
        name="receiver_side",
    )(
        stay(layer_slowness),
        stay(layer_index.reshape(HIGH, LANES)),
        stay(field.reshape(2, BLOCK, NX)),
        stay(twiddles),
        stay(weights),
        stay(props),
    )
    arrived = lax.all_to_all(chunks.reshape(groups, 16, LANES), "row", 0, 0, tiled=True)
    parts, image = pl.pallas_call(
        second_kernel,
        out_shape=(keep(2, 2, HIGH, BLOCK, LANES), pltpu.HBM((total, BLOCK, HOFF), jnp.float32)),
        in_specs=[smem] + [vmem] * 5,
        out_specs=(vmem, hbm),
        scratch_shapes=[
            pltpu.VMEM((2, 2, HIGH, 16, LANES), jnp.float32),
            pltpu.VMEM((BLOCK, 2 * LANES), jnp.float32),
            pltpu.SemaphoreType.DMA((total,)),
        ],
        compiler_params=params,
        cost_estimate=cost(10**9),
        name="shot_side",
    )(roots, arrived.reshape(16 * groups, LANES), corr, weights, twiddles, props)
    images = lax.all_to_all(image, "freq", 0, 0, tiled=True)
    sunk = pl.pallas_call(
        third_kernel,
        out_shape=shape(2, BLOCK, NX),
        in_specs=[vmem, vmem],
        out_specs=vmem,
        compiler_params=params,
        cost_estimate=cost(10**8),
        name="shot_side_end",
    )(near(parts), near(corr))
    image = jnp.swapaxes(jnp.sum(images, axis=0), 0, 1)
    return jnp.swapaxes(sunk, 1, 2)[:, None], image


def solution(mesh):
    return jax.shard_map(
        on_device,
        mesh=mesh,
        in_specs=(P(None, "freq", "row", None), P(), P()),
        out_specs=(P(None, "freq", None, "row"), P(None, "row")),
        check_vma=False,
    )
```

```python
import math

import jax
import jax.numpy as jnp
import ml_dtypes
import numpy as np
from jax import lax
from jax.experimental import pallas as pl
from jax.experimental.pallas import tpu as pltpu
from jax.sharding import PartitionSpec as P

HOFF = 128
NX = 2048
NL = 16
BLOCK = 32
HIGH = 16
PAIRS = 32
LANES = 128

depth_step = 0.0125
grid_step = 0.0125
slow_slow = 1.0 / 1.5
slow_fast = 1.0 / 4.5
refs = (slow_slow, slow_fast)


def split16(table):
    high = table.astype(np.float32).astype(ml_dtypes.bfloat16)
    low = (table - high.astype(np.float64)).astype(np.float32).astype(ml_dtypes.bfloat16)
    return high, low


def real_form(matrix):
    return np.block([[matrix.real, matrix.imag], [-matrix.imag, matrix.real]])


def fourier(count):
    index = np.arange(count)
    return np.exp(-2j * math.pi * (index[:, None] * index[None, :] % count) / count)


def receiver_weights():
    forward = fourier(LANES)
    return np.stack([split16(forward.real), split16(-forward.imag)], axis=1)


def shot_weights():
    forward = fourier(64)
    same = np.eye(2)
    into = np.einsum("bsk,hg->bhsgk", forward.reshape(2, 32, 64), same).reshape(LANES, LANES)
    back = np.einsum("ks,hg->hkgs", forward.conj(), same).reshape(LANES, LANES)
    out = []
    for high, low in (split16(real_form(into)), split16(real_form(back))):
        out.append(np.concatenate([high, high, low]))
    return np.stack(out)


def twiddle_rows(count, position):
    angle = -2.0 * math.pi * np.arange(count)[:, None] * position[None, :] / NX
    return np.stack([np.cos(angle), np.sin(angle)]).astype(np.float32)


def shot_twiddles():
    lane = np.arange(LANES)
    into = twiddle_rows(PAIRS, lane // 64 * 32 + lane % 32)
    back = twiddle_rows(PAIRS, lane % 64)
    roots = twiddle_rows(PAIRS, np.full(LANES, -NX // PAIRS))
    return np.stack([into, back, roots])


def omega_of(index, total):
    return 2.0 * math.pi * (5.0 + 30.0 * (index + 0.5) / total)


def propagators(total):
    index = np.arange(NX)
    knum = np.where(index < NX // 2, index, index - NX) * (2.0 * math.pi / (NX * grid_step))
    wide = np.zeros((total, 2, 2, HIGH, LANES), np.float32)
    paired = np.zeros((total, 2, 2, PAIRS, LANES), np.float32)
    for f in range(total):
        for j in range(2):
            quad = (omega_of(f, total) * refs[j]) ** 2 - knum**2
            mag = np.exp(-depth_step * np.sqrt(np.maximum(-quad, 0.0)))
            phase = -depth_step * np.sqrt(np.maximum(quad, 0.0))
            for c, values in enumerate((mag * np.cos(phase), mag * np.sin(phase))):
                wide[f, j, c] = values.reshape(LANES, HIGH).T
                paired[f, j, c] = np.tile(values.reshape(64, PAIRS).T, (1, 2))
    return wide, paired


def add(a, b):
    return a[0] + b[0], a[1] + b[1]


def sub(a, b):
    return a[0] - b[0], a[1] - b[1]


def mul(a, b):
    return a[0] * b[0] - a[1] * b[1], a[0] * b[1] + a[1] * b[0]


def mul_conj(a, b):
    return a[0] * b[0] + a[1] * b[1], a[1] * b[0] - a[0] * b[1]


def fft4(x, sign):
    t0, t1 = add(x[0], x[2]), sub(x[0], x[2])
    t2, t3 = add(x[1], x[3]), sub(x[1], x[3])
    up = (t1[0] - t3[1], t1[1] + t3[0])
    down = (t1[0] + t3[1], t1[1] - t3[0])
    if sign < 0:
        up, down = down, up
    return [add(t0, t2), up, sub(t0, t2), down]


def turn(x, step, count, sign):
    eighths = 8 * (step % count)
    if eighths == 0:
        return x
    if eighths == 2 * count:
        return (x[1], -x[0]) if sign < 0 else (-x[1], x[0])
    if eighths == count:
        root = math.sqrt(0.5)
        if sign < 0:
            return (x[0] + x[1]) * root, (x[1] - x[0]) * root
        return (x[0] - x[1]) * root, (x[1] + x[0]) * root
    angle = sign * 2.0 * math.pi * step / count
    return mul(x, (math.cos(angle), math.sin(angle)))


def fft(x, sign):
    count = len(x)
    if count == 1:
        return x
    if count == 2:
        return [add(x[0], x[1]), sub(x[0], x[1])]
    if count == 4:
        return fft4(x, sign)
    first = 4 if count > 8 else 2
    second = count // first
    parts = [fft([x[second * m + n] for m in range(first)], sign) for n in range(second)]
    out = [None] * count
    for k in range(first):
        column = fft([turn(parts[n][k], n * k, count, sign) for n in range(second)], sign)
        for m in range(second):
            out[k + first * m] = column[m]
    return out


def halves(x):
    high = x.astype(jnp.bfloat16)
    return high, (x - high.astype(jnp.float32)).astype(jnp.bfloat16)


def dot3(x, w):
    high, low = halves(x)
    return jnp.dot(jnp.concatenate([high, low, high], axis=1), w, preferred_element_type=jnp.float32)


def row(ref, i):
    return ref[pl.ds(i, 1), :]


def scatter_up(x, tw, out_ref, rows, at):
    for k, tile in enumerate(fft(x, -1)):
        turned = mul(tile, (row(tw.at[0], k), row(tw.at[1], k)))
        for c in range(2):
            out_ref[rows * k + at : rows * k + at + 8, LANES * c : LANES * (c + 1)] = turned[c]


def middle(in_ref, rows, w_ref, e_ref, tw, out_ref):
    count = in_ref.shape[0] // rows
    spec = dot3(in_ref[...], w_ref[0])
    for j in range(2):
        moved = []
        for k in range(count):
            part = spec[k * rows : (k + 1) * rows]
            e = (row(e_ref.at[0, j, 0], k), row(e_ref.at[0, j, 1], k))
            moved.append(jnp.concatenate(mul((part[:, :LANES], part[:, LANES:]), e), axis=1))
        back = dot3(jnp.concatenate(moved, axis=0), w_ref[1])
        for k in range(count):
            part = back[k * rows : (k + 1) * rows]
            turn_back = (row(tw.at[0], k), row(tw.at[1], k))
            turned = mul_conj((part[:, :LANES], part[:, LANES:]), turn_back)
            for c in range(2):
                out_ref[j, c, k] = turned[c]


def gather_up(tiles_of, corr_of):
    result = None
    for j in range(2):
        terms = [mul(v, corr_of(j, a)) for a, v in enumerate(fft(tiles_of(j), 1))]
        result = terms if result is None else [add(r, t) for r, t in zip(result, terms)]
    return result


def corrections(index, slow_ref, omega):
    slowness = jnp.zeros(index.shape, jnp.float32)
    for layer in range(NL):
        slowness = jnp.where(index == layer, slow_ref[layer], slowness)
    upper = (slow_slow - slowness) / (slow_slow - slow_fast)
    weights = (1.0 - upper, upper)
    out = []
    for j in range(2):
        angle = -omega * depth_step * (slowness - refs[j])
        scale = weights[j] * (1.0 / NX)
        out.append((scale * jnp.cos(angle), scale * jnp.sin(angle)))
    return out


def exchange(x, y, mask, width):
    return (
        jnp.where(mask, x, pltpu.roll(y, width, 1)),
        jnp.where(mask, pltpu.roll(x, LANES - width, 1), y),
    )


def lanes_of(rows):
    return lax.broadcasted_iota(jnp.int32, (rows, LANES), 1)


def first_kernel(
    total, slow_hbm, index_hbm, field_hbm, tw_hbm, w_hbm, e_hbm, out_ref, corr_ref,
    slow_ref, index_ref, field_ref, tw_ref, wave_ref, e_ref, own_ref, w_ref, mid_ref, back_ref, sunk, sems,
):
    freq = lax.axis_index("freq")
    pairs = [
        (slow_hbm, slow_ref),
        (index_hbm, index_ref),
        (tw_hbm, tw_ref),
        (w_hbm, wave_ref),
        (e_hbm.at[pl.ds(freq, 1)], e_ref),
    ]
    for at in range(0, BLOCK, 8):
        pairs.append((field_hbm.at[:, pl.ds(at, 8)], field_ref.at[:, pl.ds(at, 8)]))
    copies = [pltpu.make_async_copy(s, d, sems.at[i]) for i, (s, d) in enumerate(pairs)]
    for copy in copies:
        copy.start()
    copies[0].wait()
    copies[1].wait()
    omega = 2.0 * math.pi * (5.0 + 30.0 * (freq.astype(jnp.float32) + 0.5) / total)
    left = lanes_of(HIGH) < 64
    for j, values in enumerate(corrections(index_ref[...], slow_ref, omega)):
        for c in range(2):
            own_ref[j, c] = values[c]
            other = pltpu.roll(values[c], 64, 1)
            corr_ref[j, c, 0] = jnp.where(left, values[c], other)
            corr_ref[j, c, 1] = jnp.where(left, other, values[c])
    copies[2].wait()
    copies[3].wait()
    copies[4].wait()
    for part, level in enumerate((0, 0, 1)):
        for way, sign in enumerate((1, -1)):
            cos, sin = wave_ref[level, 0], wave_ref[level, 1] * sign
            for at, blocks in enumerate(((cos, -sin), (sin, cos))):
                for c in range(2):
                    base = 256 * part + LANES * at
                    w_ref[way, base : base + LANES, LANES * c : LANES * (c + 1)] = blocks[c]
    for i, at in enumerate(range(0, BLOCK, 8)):
        copies[5 + i].wait()
        x = [
            tuple(field_ref[c, at : at + 8, LANES * a : LANES * (a + 1)] for c in range(2))
            for a in range(HIGH)
        ]
        scatter_up(x, tw_ref, mid_ref, BLOCK, at)
    middle(mid_ref, BLOCK, w_ref, e_ref, tw_ref, back_ref)
    for at in range(0, BLOCK, 8):
        u = gather_up(
            lambda j: [tuple(back_ref[j, c, k, at : at + 8, :] for c in range(2)) for k in range(HIGH)],
            lambda j, a: (row(own_ref.at[j, 0], a), row(own_ref.at[j, 1], a)),
        )
        for a in range(HIGH):
            for c in range(2):
                base = c * 64 + (a % 2) * 32 + at
                sunk[a // 2, base : base + 8, :] = u[a][c]
    even = (lanes_of(16) & 63) < 32
    for p in range(HIGH // 2):
        turned = sunk[p].T
        for q in range(4):
            first, second = exchange(turned[32 * q : 32 * q + 16], turned[32 * q + 16 : 32 * q + 32], even, 32)
            out_ref[p * 128 + 16 * q : p * 128 + 16 * q + 16, :] = first
            out_ref[p * 128 + 64 + 16 * q : p * 128 + 80 + 16 * q, :] = second


def second_kernel(in_ref, corr_ref, w_ref, tw_ref, e_all, parts_ref, image_hbm, mid_ref, image_ref, sems):
    e_ref = e_all.at[pl.ds(lax.axis_index("freq"), 1)]
    left = lanes_of(8) < 64
    for at in (0, 8):
        x = []
        for m in range(PAIRS):
            first, second = (in_ref[32 * m + 16 * i + at : 32 * m + 16 * i + at + 8, :] for i in range(2))
            x.append(exchange(first, second, left, 64))
        scatter_up(x, tw_ref.at[0], mid_ref, 16, at)
    middle(mid_ref, 16, w_ref, e_ref, tw_ref.at[1], parts_ref)
    start = (lax.axis_index("row") * BLOCK + NX - HOFF // 2) & (NX - 1)
    offset = start & 63
    strips = []
    for i in range(3):
        m = ((start >> 6) + i) & (PAIRS - 1)
        strip = None
        for j in range(2):
            here = None
            for k in range(PAIRS):
                at = (m * k) & (PAIRS - 1)
                root = (row(tw_ref.at[2, 0], at), row(tw_ref.at[2, 1], at))
                term = mul((parts_ref[j, 0, k], parts_ref[j, 1, k]), root)
                here = term if here is None else add(here, term)
            c = (row(corr_ref.at[j, 0, m & 1], m >> 1), row(corr_ref.at[j, 1, m & 1], m >> 1))
            term = here[0] * c[0] - here[1] * c[1]
            strip = term if strip is None else strip + term
        strips.append(strip)
    left = lanes_of(16) < 64
    bands = zip(exchange(strips[0], strips[1], left, 64), (strips[2], pltpu.roll(strips[2], 64, 1)))
    line = lax.broadcasted_iota(jnp.int32, (8, LANES), 0)
    lane = lanes_of(8)
    for h, (near, far) in enumerate(bands):
        for at in (0, 8):
            image = None
            for i in range(8):
                width = offset + 16 * h + at + i
                back = (LANES - width) & (LANES - 1)
                moved = jnp.where(
                    lane < LANES - width,
                    pltpu.roll(near[at : at + 8], back, 1),
                    pltpu.roll(far[at : at + 8], back, 1),
                )
                image = moved if image is None else jnp.where(line == i, moved, image)
            image_ref[16 * h + at : 16 * h + at + 8, :] = image
    copies = [
        pltpu.make_async_copy(image_ref, image_hbm.at[f], sems.at[f]) for f in range(image_hbm.shape[0])
    ]
    for copy in copies:
        copy.start()
    for copy in copies:
        copy.wait()


def third_kernel(parts_ref, corr_ref, out_ref):
    left = lanes_of(8) < 64
    for at in (0, 8):
        u = gather_up(
            lambda j: [tuple(parts_ref[j, c, k, at : at + 8, :] for c in range(2)) for k in range(PAIRS)],
            lambda j, m: tuple(row(corr_ref.at[j, c, m % 2], m // 2) for c in range(2)),
        )
        for a in range(HIGH):
            for c in range(2):
                for h, tile in enumerate(exchange(u[2 * a][c], u[2 * a + 1][c], left, 64)):
                    out_ref[c, 16 * h + at : 16 * h + at + 8, LANES * a : LANES * (a + 1)] = tile


def on_device(field, layer_index, layer_slowness):
    total = lax.axis_size("freq")
    groups = lax.axis_size("row")
    wide, paired = (jnp.asarray(table) for table in propagators(total))
    twiddles = jnp.asarray(twiddle_rows(HIGH, np.arange(LANES)))
    shape = lambda *dims: jax.ShapeDtypeStruct(dims, jnp.float32)
    keep = lambda *dims: pltpu.VMEM(dims, jnp.float32)
    vmem = pl.BlockSpec(memory_space=pltpu.VMEM)
    hbm = pl.BlockSpec(memory_space=pltpu.HBM)
    stay = lambda x: pltpu.with_memory_space_constraint(x, pltpu.HBM)
    near = lambda x: pltpu.with_memory_space_constraint(x, pltpu.VMEM)
    params = pltpu.CompilerParams(vmem_limit_bytes=32 * 2**20)
    cost = lambda n: pl.CostEstimate(flops=n, bytes_accessed=2**20, transcendentals=0)
    chunks, corr = pl.pallas_call(
        lambda *a: first_kernel(total, *a),
        out_shape=(keep(16 * groups, LANES), keep(2, 2, 2, HIGH, LANES)),
        in_specs=[hbm] * 6,
        out_specs=(vmem, vmem),
        scratch_shapes=[
            pltpu.SMEM((NL,), jnp.float32),
            pltpu.VMEM((HIGH, LANES), jnp.int32),
            pltpu.VMEM((2, BLOCK, NX), jnp.float32),
            pltpu.VMEM((2, HIGH, LANES), jnp.float32),
            pltpu.VMEM((2, 2, LANES, LANES), jnp.bfloat16),
            pltpu.VMEM((1, 2, 2, HIGH, LANES), jnp.float32),
            pltpu.VMEM((2, 2, HIGH, LANES), jnp.float32),
            pltpu.VMEM((2, 768, 256), jnp.bfloat16),
            pltpu.VMEM((512, 256), jnp.float32),
            pltpu.VMEM((2, 2, HIGH, BLOCK, LANES), jnp.float32),
            pltpu.VMEM((HIGH // 2, LANES, LANES), jnp.float32),
            pltpu.SemaphoreType.DMA((9,)),
        ],
        compiler_params=params,
        cost_estimate=cost(10**9),
        name="receiver_side",
    )(
        stay(layer_slowness),
        stay(layer_index.reshape(HIGH, LANES)),
        stay(field.reshape(2, BLOCK, NX)),
        stay(twiddles),
        stay(jnp.asarray(receiver_weights())),
        stay(wide),
    )
    arrived = lax.all_to_all(chunks.reshape(groups, 16, LANES), "row", 0, 0, tiled=True)
    parts, image = pl.pallas_call(
        second_kernel,
        out_shape=(keep(2, 2, PAIRS, 16, LANES), pltpu.HBM((total, BLOCK, HOFF), jnp.float32)),
        in_specs=[vmem] * 5,
        out_specs=(vmem, hbm),
        scratch_shapes=[
            pltpu.VMEM((512, 256), jnp.float32),
            pltpu.VMEM((BLOCK, LANES), jnp.float32),
            pltpu.SemaphoreType.DMA((total,)),
        ],
        compiler_params=params,
        cost_estimate=cost(10**9),
        name="shot_side",
    )(
        near(arrived.reshape(16 * groups, LANES)),
        near(corr),
        jnp.asarray(shot_weights()),
        jnp.asarray(shot_twiddles()),
        paired,
    )
    images = lax.all_to_all(image, "freq", 0, 0, tiled=True)
    sunk = pl.pallas_call(
        third_kernel,
        out_shape=shape(2, BLOCK, NX),
        in_specs=[vmem, vmem],
        out_specs=vmem,
        compiler_params=params,
        cost_estimate=cost(10**8),
        name="shot_side_end",
    )(near(parts), near(corr))
    image = jnp.swapaxes(jnp.sum(images, axis=0), 0, 1)
    return jnp.swapaxes(sunk, 1, 2)[:, None], image


def solution(mesh):
    return jax.shard_map(
        on_device,
        mesh=mesh,
        in_specs=(P(None, "freq", "row", None), P(), P()),
        out_specs=(P(None, "freq", None, "row"), P(None, "row")),
        check_vma=False,
    )
```

```python
import math

import jax
import jax.numpy as jnp
import ml_dtypes
import numpy as np
from jax import lax
from jax.experimental import pallas as pl
from jax.experimental.pallas import tpu as pltpu
from jax.sharding import PartitionSpec as P

HOFF = 128
NX = 2048
NL = 16
BLOCK = 32
HIGH = 16
PAIRS = 32
LANES = 128

depth_step = 0.0125
grid_step = 0.0125
slow_slow = 1.0 / 1.5
slow_fast = 1.0 / 4.5
refs = (slow_slow, slow_fast)


def split16(table):
    high = table.astype(np.float32).astype(ml_dtypes.bfloat16)
    low = (table - high.astype(np.float64)).astype(np.float32).astype(ml_dtypes.bfloat16)
    return high, low


def real_form(matrix):
    return np.block([[matrix.real, matrix.imag], [-matrix.imag, matrix.real]])


def fourier(count):
    index = np.arange(count)
    return np.exp(-2j * math.pi * (index[:, None] * index[None, :] % count) / count)


def receiver_weights():
    forward = fourier(LANES)
    return np.stack([split16(forward.real), split16(-forward.imag)], axis=1)


def shot_weights():
    forward = fourier(64)
    same = np.eye(2)
    into = np.einsum("bsk,hg->bhsgk", forward.reshape(2, 32, 64), same).reshape(LANES, LANES)
    back = np.einsum("ks,hg->hkgs", forward.conj(), same).reshape(LANES, LANES)
    out = []
    for high, low in (split16(real_form(into)), split16(real_form(back))):
        out.append(np.concatenate([high, high, low]))
    return np.stack(out)


def twiddle_rows(count, position):
    angle = -2.0 * math.pi * np.arange(count)[:, None] * position[None, :] / NX
    return np.stack([np.cos(angle), np.sin(angle)]).astype(np.float32)


def shot_twiddles():
    lane = np.arange(LANES)
    into = twiddle_rows(PAIRS, lane // 64 * 32 + lane % 32)
    back = twiddle_rows(PAIRS, lane % 64)
    return np.stack([into, back])


def window_twiddles():
    lane = np.arange(LANES) % 64
    return np.stack([twiddle_rows(PAIRS, lane + 64 * m) for m in range(PAIRS)])


def window_start():
    return (lax.axis_index("row") * BLOCK + NX - HOFF // 2) & (NX - 1)


def omega_of(index, total):
    return 2.0 * math.pi * (5.0 + 30.0 * (index + 0.5) / total)


def propagators(total):
    index = np.arange(NX)
    knum = np.where(index < NX // 2, index, index - NX) * (2.0 * math.pi / (NX * grid_step))
    wide = np.zeros((total, 2, 2, HIGH, LANES), np.float32)
    paired = np.zeros((total, 2, 2, PAIRS, LANES), np.float32)
    for f in range(total):
        for j in range(2):
            quad = (omega_of(f, total) * refs[j]) ** 2 - knum**2
            mag = np.exp(-depth_step * np.sqrt(np.maximum(-quad, 0.0)))
            phase = -depth_step * np.sqrt(np.maximum(quad, 0.0))
            for c, values in enumerate((mag * np.cos(phase), mag * np.sin(phase))):
                wide[f, j, c] = values.reshape(LANES, HIGH).T
                paired[f, j, c] = np.tile(values.reshape(64, PAIRS).T, (1, 2))
    return wide, paired


def add(a, b):
    return a[0] + b[0], a[1] + b[1]


def sub(a, b):
    return a[0] - b[0], a[1] - b[1]


def mul(a, b):
    return a[0] * b[0] - a[1] * b[1], a[0] * b[1] + a[1] * b[0]


def mul_conj(a, b):
    return a[0] * b[0] + a[1] * b[1], a[1] * b[0] - a[0] * b[1]


def fft4(x, sign):
    t0, t1 = add(x[0], x[2]), sub(x[0], x[2])
    t2, t3 = add(x[1], x[3]), sub(x[1], x[3])
    up = (t1[0] - t3[1], t1[1] + t3[0])
    down = (t1[0] + t3[1], t1[1] - t3[0])
    if sign < 0:
        up, down = down, up
    return [add(t0, t2), up, sub(t0, t2), down]


def turn(x, step, count, sign):
    eighths = 8 * (step % count)
    if eighths == 0:
        return x
    if eighths == 2 * count:
        return (x[1], -x[0]) if sign < 0 else (-x[1], x[0])
    if eighths == count:
        root = math.sqrt(0.5)
        if sign < 0:
            return (x[0] + x[1]) * root, (x[1] - x[0]) * root
        return (x[0] - x[1]) * root, (x[1] + x[0]) * root
    angle = sign * 2.0 * math.pi * step / count
    return mul(x, (math.cos(angle), math.sin(angle)))


def fft(x, sign):
    count = len(x)
    if count == 1:
        return x
    if count == 2:
        return [add(x[0], x[1]), sub(x[0], x[1])]
    if count == 4:
        return fft4(x, sign)
    first = 4 if count > 8 else 2
    second = count // first
    parts = [fft([x[second * m + n] for m in range(first)], sign) for n in range(second)]
    out = [None] * count
    for k in range(first):
        column = fft([turn(parts[n][k], n * k, count, sign) for n in range(second)], sign)
        for m in range(second):
            out[k + first * m] = column[m]
    return out


def halves(x):
    high = x.astype(jnp.bfloat16)
    return high, (x - high.astype(jnp.float32)).astype(jnp.bfloat16)


def dot3(x, w):
    high, low = halves(x)
    return jnp.dot(jnp.concatenate([high, low, high], axis=1), w, preferred_element_type=jnp.float32)


def row(ref, i):
    return ref[pl.ds(i, 1), :]


def scatter_up(x, tw, out_ref, rows, at):
    for k, tile in enumerate(fft(x, -1)):
        turned = mul(tile, (row(tw.at[0], k), row(tw.at[1], k)))
        for c in range(2):
            out_ref[rows * k + at : rows * k + at + 8, LANES * c : LANES * (c + 1)] = turned[c]


def middle(in_ref, rows, w_ref, e_ref, tw, out_ref):
    count = in_ref.shape[0] // rows
    spec = dot3(in_ref[...], w_ref[0])
    for j in range(2):
        moved = []
        for k in range(count):
            part = spec[k * rows : (k + 1) * rows]
            e = (row(e_ref.at[0, j, 0], k), row(e_ref.at[0, j, 1], k))
            moved.append(jnp.concatenate(mul((part[:, :LANES], part[:, LANES:]), e), axis=1))
        back = dot3(jnp.concatenate(moved, axis=0), w_ref[1])
        tiles = []
        for k in range(count):
            part = back[k * rows : (k + 1) * rows]
            tiles.append((part[:, :LANES], part[:, LANES:]))
            turned = mul_conj(tiles[k], (row(tw.at[0], k), row(tw.at[1], k)))
            for c in range(2):
                out_ref[j, c, k] = turned[c]
        yield j, tiles


def window_tiles(tiles, tw):
    sums = [None] * 3
    for k in range(8):
        part = [mul_conj(tiles[k + n], (row(tw.at[0], k + n), row(tw.at[1], k + n))) for n in range(0, 32, 8)]
        even = add(part[0], part[2]), add(part[1], part[3])
        odd = sub(part[0], part[2]), sub(part[1], part[3])
        odd = (odd[0][0] - odd[1][1], odd[0][1] + odd[1][0])
        terms = (add(*even), turn(odd, k, 32, 1), turn(sub(*even), k, 16, 1))
        sums = [t if p is None else add(p, t) for p, t in zip(sums, terms)]
    return sums


def gather_up(tiles_of, corr_of):
    result = None
    for j in range(2):
        terms = [mul(v, corr_of(j, a)) for a, v in enumerate(fft(tiles_of(j), 1))]
        result = terms if result is None else [add(r, t) for r, t in zip(result, terms)]
    return result


def corrections(index, slow_ref, omega):
    slowness = jnp.zeros(index.shape, jnp.float32)
    for layer in range(NL):
        slowness = jnp.where(index == layer, slow_ref[layer], slowness)
    upper = (slow_slow - slowness) / (slow_slow - slow_fast)
    weights = (1.0 - upper, upper)
    out = []
    for j in range(2):
        angle = -omega * depth_step * (slowness - refs[j])
        scale = weights[j] * (1.0 / NX)
        out.append((scale * jnp.cos(angle), scale * jnp.sin(angle)))
    return out


def exchange(x, y, mask, width):
    return (
        jnp.where(mask, x, pltpu.roll(y, width, 1)),
        jnp.where(mask, pltpu.roll(x, LANES - width, 1), y),
    )


def place(block):
    return (3 * (block // 8) % 8) * 8 + block % 8


def row_order(groups):
    order = [0] * groups
    for block in range(groups):
        order[place(block)] = block
    return order


def freq_order(total):
    return [3 * i % total for i in range(total)]


def lanes_of(rows):
    return lax.broadcasted_iota(jnp.int32, (rows, LANES), 1)


def first_kernel(
    total, slow_hbm, index_hbm, field_hbm, tw_hbm, w_hbm, e_hbm, window_hbm, out_ref, corr_ref, window_ref,
    slow_ref, index_ref, field_ref, tw_ref, wave_ref, e_ref, own_ref, w_ref, mid_ref, back_ref, sunk, sems,
):
    freq = lax.axis_index("freq")
    pairs = [
        (slow_hbm, slow_ref),
        (index_hbm, index_ref),
        (tw_hbm, tw_ref),
        (w_hbm, wave_ref),
        (e_hbm.at[pl.ds(freq, 1)], e_ref),
    ]
    for at in range(0, BLOCK, 8):
        pairs.append((field_hbm.at[:, pl.ds(at, 8)], field_ref.at[:, pl.ds(at, 8)]))
    pairs.append((window_hbm.at[window_start() >> 6], window_ref))
    copies = [pltpu.make_async_copy(s, d, sems.at[i]) for i, (s, d) in enumerate(pairs)]
    for copy in copies:
        copy.start()
    copies[0].wait()
    copies[1].wait()
    omega = 2.0 * math.pi * (5.0 + 30.0 * (freq.astype(jnp.float32) + 0.5) / total)
    left = lanes_of(HIGH) < 64
    for j, values in enumerate(corrections(index_ref[...], slow_ref, omega)):
        for c in range(2):
            own_ref[j, c] = values[c]
            other = pltpu.roll(values[c], 64, 1)
            corr_ref[j, c, 0] = jnp.where(left, values[c], other)
            corr_ref[j, c, 1] = jnp.where(left, other, values[c])
    copies[2].wait()
    copies[3].wait()
    copies[4].wait()
    for part, level in enumerate((0, 0, 1)):
        for way, sign in enumerate((1, -1)):
            cos, sin = wave_ref[level, 0], wave_ref[level, 1] * sign
            for at, blocks in enumerate(((cos, -sin), (sin, cos))):
                for c in range(2):
                    base = 256 * part + LANES * at
                    w_ref[way, base : base + LANES, LANES * c : LANES * (c + 1)] = blocks[c]
    for i, at in enumerate(range(0, BLOCK, 8)):
        copies[5 + i].wait()
        x = [
            tuple(field_ref[c, at : at + 8, LANES * a : LANES * (a + 1)] for c in range(2))
            for a in range(HIGH)
        ]
        scatter_up(x, tw_ref, mid_ref, BLOCK, at)
    for _ in middle(mid_ref, BLOCK, w_ref, e_ref, tw_ref, back_ref):
        pass
    copies[9].wait()
    for at in range(0, BLOCK, 8):
        u = gather_up(
            lambda j: [tuple(back_ref[j, c, k, at : at + 8, :] for c in range(2)) for k in range(HIGH)],
            lambda j, a: (row(own_ref.at[j, 0], a), row(own_ref.at[j, 1], a)),
        )
        for a in range(HIGH):
            for c in range(2):
                base = c * 64 + (a % 2) * 32 + at
                sunk[a // 2, base : base + 8, :] = u[a][c]
    even = (lanes_of(16) & 63) < 32
    for p in range(HIGH // 2):
        turned = sunk[p].T
        for q in range(4):
            first, second = exchange(turned[32 * q : 32 * q + 16], turned[32 * q + 16 : 32 * q + 32], even, 32)
            for block, chunk in ((8 * p + q, first), (8 * p + 4 + q, second)):
                out_ref[16 * place(block) : 16 * place(block) + 16, :] = chunk


def second_kernel(in_ref, corr_ref, window_ref, w_ref, tw_ref, e_all, parts_ref, image_hbm, mid_ref, image_ref, sems):
    e_ref = e_all.at[pl.ds(lax.axis_index("freq"), 1)]
    left = lanes_of(8) < 64
    for at in (0, 8):
        x = []
        for m in range(PAIRS):
            first, second = (
                in_ref[16 * place(2 * m + i) + at : 16 * place(2 * m + i) + at + 8, :] for i in range(2)
            )
            x.append(exchange(first, second, left, 64))
        scatter_up(x, tw_ref.at[0], mid_ref, 16, at)
    start = window_start()
    offset = start & 63
    strips = [None] * 3
    for j, tiles in middle(mid_ref, 16, w_ref, e_ref, tw_ref.at[1], parts_ref):
        for i, here in enumerate(window_tiles(tiles, window_ref)):
            m = ((start >> 6) + i) & (PAIRS - 1)
            c = (row(corr_ref.at[j, 0, m & 1], m >> 1), row(corr_ref.at[j, 1, m & 1], m >> 1))
            term = here[0] * c[0] - here[1] * c[1]
            strips[i] = term if j == 0 else strips[i] + term
    left = lanes_of(16) < 64
    bands = zip(exchange(strips[0], strips[1], left, 64), (strips[2], pltpu.roll(strips[2], 64, 1)))
    line = lax.broadcasted_iota(jnp.int32, (8, LANES), 0)
    lane = lanes_of(8)
    for h, (near, far) in enumerate(bands):
        for at in (0, 8):
            image = None
            for i in range(8):
                width = offset + 16 * h + at + i
                back = (LANES - width) & (LANES - 1)
                moved = jnp.where(
                    lane < LANES - width,
                    pltpu.roll(near[at : at + 8], back, 1),
                    pltpu.roll(far[at : at + 8], back, 1),
                )
                image = moved if image is None else jnp.where(line == i, moved, image)
            image_ref[16 * h + at : 16 * h + at + 8, :] = image
    copies = [
        pltpu.make_async_copy(image_ref, image_hbm.at[f], sems.at[f]) for f in range(image_hbm.shape[0])
    ]
    for copy in copies:
        copy.start()
    for copy in copies:
        copy.wait()


def third_kernel(parts_ref, corr_ref, out_ref):
    left = lanes_of(8) < 64
    for at in (0, 8):
        u = gather_up(
            lambda j: [tuple(parts_ref[j, c, k, at : at + 8, :] for c in range(2)) for k in range(PAIRS)],
            lambda j, m: tuple(row(corr_ref.at[j, c, m % 2], m // 2) for c in range(2)),
        )
        for a in range(HIGH):
            for c in range(2):
                for h, tile in enumerate(exchange(u[2 * a][c], u[2 * a + 1][c], left, 64)):
                    out_ref[c, 16 * h + at : 16 * h + at + 8, LANES * a : LANES * (a + 1)] = tile


def on_device(field, layer_index, layer_slowness):
    total = lax.axis_size("freq")
    groups = lax.axis_size("row")
    wide, paired = (jnp.asarray(table) for table in propagators(total))
    twiddles = jnp.asarray(twiddle_rows(HIGH, np.arange(LANES)))
    shape = lambda *dims: jax.ShapeDtypeStruct(dims, jnp.float32)
    keep = lambda *dims: pltpu.VMEM(dims, jnp.float32)
    vmem = pl.BlockSpec(memory_space=pltpu.VMEM)
    hbm = pl.BlockSpec(memory_space=pltpu.HBM)
    stay = lambda x: pltpu.with_memory_space_constraint(x, pltpu.HBM)
    near = lambda x: pltpu.with_memory_space_constraint(x, pltpu.VMEM)
    params = pltpu.CompilerParams(vmem_limit_bytes=32 * 2**20)
    cost = lambda n: pl.CostEstimate(flops=n, bytes_accessed=2**20, transcendentals=0)
    chunks, corr, window = pl.pallas_call(
        lambda *a: first_kernel(total, *a),
        out_shape=(keep(16 * groups, LANES), keep(2, 2, 2, HIGH, LANES), keep(2, PAIRS, LANES)),
        in_specs=[hbm] * 7,
        out_specs=(vmem, vmem, vmem),
        scratch_shapes=[
            pltpu.SMEM((NL,), jnp.float32),
            pltpu.VMEM((HIGH, LANES), jnp.int32),
            pltpu.VMEM((2, BLOCK, NX), jnp.float32),
            pltpu.VMEM((2, HIGH, LANES), jnp.float32),
            pltpu.VMEM((2, 2, LANES, LANES), jnp.bfloat16),
            pltpu.VMEM((1, 2, 2, HIGH, LANES), jnp.float32),
            pltpu.VMEM((2, 2, HIGH, LANES), jnp.float32),
            pltpu.VMEM((2, 768, 256), jnp.bfloat16),
            pltpu.VMEM((512, 256), jnp.float32),
            pltpu.VMEM((2, 2, HIGH, BLOCK, LANES), jnp.float32),
            pltpu.VMEM((HIGH // 2, LANES, LANES), jnp.float32),
            pltpu.SemaphoreType.DMA((10,)),
        ],
        compiler_params=params,
        cost_estimate=cost(10**9),
        name="receiver_side",
    )(
        stay(layer_slowness),
        stay(layer_index.reshape(HIGH, LANES)),
        stay(field.reshape(2, BLOCK, NX)),
        stay(twiddles),
        stay(jnp.asarray(receiver_weights())),
        stay(wide),
        stay(jnp.asarray(window_twiddles())),
    )
    arrived = lax.all_to_all(chunks.reshape(groups, 16, LANES), "row", 0, 0, tiled=True, axis_index_groups=[row_order(groups)])
    parts, image = pl.pallas_call(
        second_kernel,
        out_shape=(keep(2, 2, PAIRS, 16, LANES), pltpu.HBM((total, BLOCK, HOFF), jnp.float32)),
        in_specs=[vmem] * 6,
        out_specs=(vmem, hbm),
        scratch_shapes=[
            pltpu.VMEM((512, 256), jnp.float32),
            pltpu.VMEM((BLOCK, LANES), jnp.float32),
            pltpu.SemaphoreType.DMA((total,)),
        ],
        compiler_params=params,
        cost_estimate=cost(10**9),
        name="shot_side",
    )(
        near(arrived.reshape(16 * groups, LANES)),
        near(corr),
        near(window),
        jnp.asarray(shot_weights()),
        jnp.asarray(shot_twiddles()),
        paired,
    )
    images = lax.all_to_all(image, "freq", 0, 0, tiled=True, axis_index_groups=[freq_order(total)])
    sunk = pl.pallas_call(
        third_kernel,
        out_shape=shape(2, BLOCK, NX),
        in_specs=[vmem, vmem],
        out_specs=vmem,
        compiler_params=params,
        cost_estimate=cost(10**8),
        name="shot_side_end",
    )(near(parts), near(corr))
    image = jnp.swapaxes(jnp.sum(images, axis=0), 0, 1)
    return jnp.swapaxes(sunk, 1, 2)[:, None], image


def solution(mesh):
    return jax.shard_map(
        on_device,
        mesh=mesh,
        in_specs=(P(None, "freq", "row", None), P(), P()),
        out_specs=(P(None, "freq", None, "row"), P(None, "row")),
        check_vma=False,
    )
```

```python
import math

import jax
import jax.numpy as jnp
import ml_dtypes
import numpy as np
from jax import lax
from jax.experimental import pallas as pl
from jax.experimental.pallas import tpu as pltpu
from jax.sharding import PartitionSpec as P

HOFF = 128
NX = 2048
NL = 16
BLOCK = 32
HIGH = 16
PAIRS = 32
LANES = 128

depth_step = 0.0125
grid_step = 0.0125
slow_slow = 1.0 / 1.5
slow_fast = 1.0 / 4.5
refs = (slow_slow, slow_fast)


def split16(table):
    high = table.astype(np.float32).astype(ml_dtypes.bfloat16)
    low = (table - high.astype(np.float64)).astype(np.float32).astype(ml_dtypes.bfloat16)
    return high, low


def real_form(matrix):
    return np.block([[matrix.real, matrix.imag], [-matrix.imag, matrix.real]])


def fourier(count):
    index = np.arange(count)
    return np.exp(-2j * math.pi * (index[:, None] * index[None, :] % count) / count)


def receiver_weights():
    forward = fourier(LANES)
    return np.stack([split16(forward.real), split16(-forward.imag)], axis=1)


def shot_weights():
    forward = fourier(64)
    same = np.eye(2)
    into = np.einsum("bsk,hg->bhsgk", forward.reshape(2, 32, 64), same).reshape(LANES, LANES)
    back = np.einsum("ks,hg->hkgs", forward.conj(), same).reshape(LANES, LANES)
    out = []
    for high, low in (split16(real_form(into)), split16(real_form(back))):
        out.append(np.concatenate([high, high, low]))
    return np.stack(out)


def twiddle_rows(count, position):
    angle = -2.0 * math.pi * np.arange(count)[:, None] * position[None, :] / NX
    return np.stack([np.cos(angle), np.sin(angle)]).astype(np.float32)


def shot_twiddles():
    lane = np.arange(LANES)
    into = twiddle_rows(PAIRS, lane // 64 * 32 + lane % 32)
    back = twiddle_rows(PAIRS, lane % 64)
    return np.stack([into, back])


def window_twiddles():
    lane = np.arange(LANES) % 64
    return np.stack([twiddle_rows(PAIRS, lane + 64 * m) for m in range(PAIRS)])


def window_start():
    return (lax.axis_index("row") * BLOCK + NX - HOFF // 2) & (NX - 1)


def omega_of(index, total):
    return 2.0 * math.pi * (5.0 + 30.0 * (index + 0.5) / total)


def propagators(total):
    index = np.arange(NX)
    knum = np.where(index < NX // 2, index, index - NX) * (2.0 * math.pi / (NX * grid_step))
    wide = np.zeros((total, 2, 2, HIGH, LANES), np.float32)
    paired = np.zeros((total, 2, 2, PAIRS, LANES), np.float32)
    for f in range(total):
        for j in range(2):
            quad = (omega_of(f, total) * refs[j]) ** 2 - knum**2
            mag = np.exp(-depth_step * np.sqrt(np.maximum(-quad, 0.0)))
            phase = -depth_step * np.sqrt(np.maximum(quad, 0.0))
            for c, values in enumerate((mag * np.cos(phase), mag * np.sin(phase))):
                wide[f, j, c] = values.reshape(LANES, HIGH).T
                paired[f, j, c] = np.tile(values.reshape(64, PAIRS).T, (1, 2))
    return wide, paired


def add(a, b):
    return a[0] + b[0], a[1] + b[1]


def sub(a, b):
    return a[0] - b[0], a[1] - b[1]


def mul(a, b):
    return a[0] * b[0] - a[1] * b[1], a[0] * b[1] + a[1] * b[0]


def mul_conj(a, b):
    return a[0] * b[0] + a[1] * b[1], a[1] * b[0] - a[0] * b[1]


def fft4(x, sign):
    t0, t1 = add(x[0], x[2]), sub(x[0], x[2])
    t2, t3 = add(x[1], x[3]), sub(x[1], x[3])
    up = (t1[0] - t3[1], t1[1] + t3[0])
    down = (t1[0] + t3[1], t1[1] - t3[0])
    if sign < 0:
        up, down = down, up
    return [add(t0, t2), up, sub(t0, t2), down]


def turn(x, step, count, sign):
    eighths = 8 * (step % count)
    if eighths == 0:
        return x
    if eighths == 2 * count:
        return (x[1], -x[0]) if sign < 0 else (-x[1], x[0])
    if eighths == count:
        root = math.sqrt(0.5)
        if sign < 0:
            return (x[0] + x[1]) * root, (x[1] - x[0]) * root
        return (x[0] - x[1]) * root, (x[1] + x[0]) * root
    angle = sign * 2.0 * math.pi * step / count
    return mul(x, (math.cos(angle), math.sin(angle)))


def fft(x, sign):
    count = len(x)
    if count == 1:
        return x
    if count == 2:
        return [add(x[0], x[1]), sub(x[0], x[1])]
    if count == 4:
        return fft4(x, sign)
    first = 4 if count > 8 else 2
    second = count // first
    parts = [fft([x[second * m + n] for m in range(first)], sign) for n in range(second)]
    out = [None] * count
    for k in range(first):
        column = fft([turn(parts[n][k], n * k, count, sign) for n in range(second)], sign)
        for m in range(second):
            out[k + first * m] = column[m]
    return out


def halves(x):
    high = x.astype(jnp.bfloat16)
    return high, (x - high.astype(jnp.float32)).astype(jnp.bfloat16)


def dot3(x, w):
    high, low = halves(x)
    return jnp.dot(jnp.concatenate([high, low, high], axis=1), w, preferred_element_type=jnp.float32)


def row(ref, i):
    return ref[pl.ds(i, 1), :]


def scatter_up(x, tw, out_ref, rows, at):
    for k, tile in enumerate(fft(x, -1)):
        turned = mul(tile, (row(tw.at[0], k), row(tw.at[1], k)))
        for c in range(2):
            out_ref[rows * k + at : rows * k + at + 8, LANES * c : LANES * (c + 1)] = turned[c]


def middle(in_ref, rows, w_ref, e_ref, tw, out_ref):
    count = in_ref.shape[0] // rows
    spec = dot3(in_ref[...], w_ref[0])
    for j in range(2):
        moved = []
        for k in range(count):
            part = spec[k * rows : (k + 1) * rows]
            e = (row(e_ref.at[0, j, 0], k), row(e_ref.at[0, j, 1], k))
            moved.append(jnp.concatenate(mul((part[:, :LANES], part[:, LANES:]), e), axis=1))
        back = dot3(jnp.concatenate(moved, axis=0), w_ref[1])
        tiles = []
        for k in range(count):
            part = back[k * rows : (k + 1) * rows]
            tiles.append((part[:, :LANES], part[:, LANES:]))
            turned = mul_conj(tiles[k], (row(tw.at[0], k), row(tw.at[1], k)))
            for c in range(2):
                out_ref[j, c, k] = turned[c]
        yield j, tiles


def window_tiles(tiles, tw):
    sums = [None] * 3
    for k in range(8):
        part = [mul_conj(tiles[k + n], (row(tw.at[0], k + n), row(tw.at[1], k + n))) for n in range(0, 32, 8)]
        even = add(part[0], part[2]), add(part[1], part[3])
        odd = sub(part[0], part[2]), sub(part[1], part[3])
        odd = (odd[0][0] - odd[1][1], odd[0][1] + odd[1][0])
        terms = (add(*even), turn(odd, k, 32, 1), turn(sub(*even), k, 16, 1))
        sums = [t if p is None else add(p, t) for p, t in zip(sums, terms)]
    return sums


def gather_up(tiles_of, corr_of):
    result = None
    for j in range(2):
        terms = [mul(v, corr_of(j, a)) for a, v in enumerate(fft(tiles_of(j), 1))]
        result = terms if result is None else [add(r, t) for r, t in zip(result, terms)]
    return result


def corrections(index, slow_ref, omega):
    slowness = jnp.zeros(index.shape, jnp.float32)
    for layer in range(NL):
        slowness = jnp.where(index == layer, slow_ref[layer], slowness)
    upper = (slow_slow - slowness) / (slow_slow - slow_fast)
    weights = (1.0 - upper, upper)
    out = []
    for j in range(2):
        angle = -omega * depth_step * (slowness - refs[j])
        scale = weights[j] * (1.0 / NX)
        out.append((scale * jnp.cos(angle), scale * jnp.sin(angle)))
    return out


def exchange(x, y, mask, width):
    return (
        jnp.where(mask, x, pltpu.roll(y, width, 1)),
        jnp.where(mask, pltpu.roll(x, LANES - width, 1), y),
    )


def place(block):
    return 11 * block % 64


def row_order(groups):
    order = [0] * groups
    for block in range(groups):
        order[place(block)] = block
    return order


def freq_order(total):
    return [3 * i % total for i in range(total)]


def lanes_of(rows):
    return lax.broadcasted_iota(jnp.int32, (rows, LANES), 1)


def first_kernel(
    total, slow_hbm, index_hbm, field_hbm, tw_hbm, w_hbm, e_hbm, window_hbm, out_ref, corr_ref, window_ref,
    slow_ref, index_ref, field_ref, tw_ref, wave_ref, e_ref, own_ref, w_ref, mid_ref, back_ref, sunk, sems,
):
    freq = lax.axis_index("freq")
    pairs = [
        (slow_hbm, slow_ref),
        (index_hbm, index_ref),
        (tw_hbm, tw_ref),
        (w_hbm, wave_ref),
        (e_hbm.at[pl.ds(freq, 1)], e_ref),
    ]
    for at in range(0, BLOCK, 8):
        pairs.append((field_hbm.at[:, pl.ds(at, 8)], field_ref.at[:, pl.ds(at, 8)]))
    pairs.append((window_hbm.at[window_start() >> 6], window_ref))
    copies = [pltpu.make_async_copy(s, d, sems.at[i]) for i, (s, d) in enumerate(pairs)]
    for copy in copies:
        copy.start()
    copies[0].wait()
    copies[1].wait()
    omega = 2.0 * math.pi * (5.0 + 30.0 * (freq.astype(jnp.float32) + 0.5) / total)
    left = lanes_of(HIGH) < 64
    for j, values in enumerate(corrections(index_ref[...], slow_ref, omega)):
        for c in range(2):
            own_ref[j, c] = values[c]
            other = pltpu.roll(values[c], 64, 1)
            corr_ref[j, c, 0] = jnp.where(left, values[c], other)
            corr_ref[j, c, 1] = jnp.where(left, other, values[c])
    copies[2].wait()
    copies[3].wait()
    copies[4].wait()
    for part, level in enumerate((0, 0, 1)):
        for way, sign in enumerate((1, -1)):
            cos, sin = wave_ref[level, 0], wave_ref[level, 1] * sign
            for at, blocks in enumerate(((cos, -sin), (sin, cos))):
                for c in range(2):
                    base = 256 * part + LANES * at
                    w_ref[way, base : base + LANES, LANES * c : LANES * (c + 1)] = blocks[c]
    for i, at in enumerate(range(0, BLOCK, 8)):
        copies[5 + i].wait()
        x = [
            tuple(field_ref[c, at : at + 8, LANES * a : LANES * (a + 1)] for c in range(2))
            for a in range(HIGH)
        ]
        scatter_up(x, tw_ref, mid_ref, BLOCK, at)
    for _ in middle(mid_ref, BLOCK, w_ref, e_ref, tw_ref, back_ref):
        pass
    copies[9].wait()
    for at in range(0, BLOCK, 8):
        u = gather_up(
            lambda j: [tuple(back_ref[j, c, k, at : at + 8, :] for c in range(2)) for k in range(HIGH)],
            lambda j, a: (row(own_ref.at[j, 0], a), row(own_ref.at[j, 1], a)),
        )
        for a in range(HIGH):
            for c in range(2):
                base = c * 64 + (a % 2) * 32 + at
                sunk[a // 2, base : base + 8, :] = u[a][c]
    even = (lanes_of(16) & 63) < 32
    for p in range(HIGH // 2):
        turned = sunk[p].T
        for q in range(4):
            first, second = exchange(turned[32 * q : 32 * q + 16], turned[32 * q + 16 : 32 * q + 32], even, 32)
            for block, chunk in ((8 * p + q, first), (8 * p + 4 + q, second)):
                out_ref[16 * place(block) : 16 * place(block) + 16, :] = chunk


def second_kernel(in_ref, corr_ref, window_ref, w_ref, tw_ref, e_all, parts_ref, images_ref, mid_ref, image_ref):
    e_ref = e_all.at[pl.ds(lax.axis_index("freq"), 1)]
    left = lanes_of(8) < 64
    for at in (0, 8):
        x = []
        for m in range(PAIRS):
            first, second = (
                in_ref[16 * place(2 * m + i) + at : 16 * place(2 * m + i) + at + 8, :] for i in range(2)
            )
            x.append(exchange(first, second, left, 64))
        scatter_up(x, tw_ref.at[0], mid_ref, 16, at)
    start = window_start()
    offset = start & 63
    strips = [None] * 3
    for j, tiles in middle(mid_ref, 16, w_ref, e_ref, tw_ref.at[1], parts_ref):
        for i, here in enumerate(window_tiles(tiles, window_ref)):
            m = ((start >> 6) + i) & (PAIRS - 1)
            c = (row(corr_ref.at[j, 0, m & 1], m >> 1), row(corr_ref.at[j, 1, m & 1], m >> 1))
            term = here[0] * c[0] - here[1] * c[1]
            strips[i] = term if j == 0 else strips[i] + term
    left = lanes_of(16) < 64
    bands = zip(exchange(strips[0], strips[1], left, 64), (strips[2], pltpu.roll(strips[2], 64, 1)))
    line = lax.broadcasted_iota(jnp.int32, (8, LANES), 0)
    lane = lanes_of(8)
    for h, (near, far) in enumerate(bands):
        for at in (0, 8):
            image = None
            for i in range(8):
                width = offset + 16 * h + at + i
                back = (LANES - width) & (LANES - 1)
                moved = jnp.where(
                    lane < LANES - width,
                    pltpu.roll(near[at : at + 8], back, 1),
                    pltpu.roll(far[at : at + 8], back, 1),
                )
                image = moved if image is None else jnp.where(line == i, moved, image)
            image_ref[16 * h + at : 16 * h + at + 8, :] = image
    for f in range(images_ref.shape[0]):
        images_ref[f] = image_ref[...]


def third_kernel(parts_ref, corr_ref, out_ref):
    left = lanes_of(8) < 64
    for at in (0, 8):
        u = gather_up(
            lambda j: [tuple(parts_ref[j, c, k, at : at + 8, :] for c in range(2)) for k in range(PAIRS)],
            lambda j, m: tuple(row(corr_ref.at[j, c, m % 2], m // 2) for c in range(2)),
        )
        for a in range(HIGH):
            for c in range(2):
                for h, tile in enumerate(exchange(u[2 * a][c], u[2 * a + 1][c], left, 64)):
                    out_ref[c, 16 * h + at : 16 * h + at + 8, LANES * a : LANES * (a + 1)] = tile


def on_device(field, layer_index, layer_slowness):
    total = lax.axis_size("freq")
    groups = lax.axis_size("row")
    wide, paired = (jnp.asarray(table) for table in propagators(total))
    twiddles = jnp.asarray(twiddle_rows(HIGH, np.arange(LANES)))
    shape = lambda *dims: jax.ShapeDtypeStruct(dims, jnp.float32)
    keep = lambda *dims: pltpu.VMEM(dims, jnp.float32)
    vmem = pl.BlockSpec(memory_space=pltpu.VMEM)
    hbm = pl.BlockSpec(memory_space=pltpu.HBM)
    stay = lambda x: pltpu.with_memory_space_constraint(x, pltpu.HBM)
    near = lambda x: pltpu.with_memory_space_constraint(x, pltpu.VMEM)
    params = pltpu.CompilerParams(vmem_limit_bytes=32 * 2**20)
    cost = lambda n: pl.CostEstimate(flops=n, bytes_accessed=2**20, transcendentals=0)
    chunks, corr, window = pl.pallas_call(
        lambda *a: first_kernel(total, *a),
        out_shape=(keep(16 * groups, LANES), keep(2, 2, 2, HIGH, LANES), keep(2, PAIRS, LANES)),
        in_specs=[hbm] * 7,
        out_specs=(vmem, vmem, vmem),
        scratch_shapes=[
            pltpu.SMEM((NL,), jnp.float32),
            pltpu.VMEM((HIGH, LANES), jnp.int32),
            pltpu.VMEM((2, BLOCK, NX), jnp.float32),
            pltpu.VMEM((2, HIGH, LANES), jnp.float32),
            pltpu.VMEM((2, 2, LANES, LANES), jnp.bfloat16),
            pltpu.VMEM((1, 2, 2, HIGH, LANES), jnp.float32),
            pltpu.VMEM((2, 2, HIGH, LANES), jnp.float32),
            pltpu.VMEM((2, 768, 256), jnp.bfloat16),
            pltpu.VMEM((512, 256), jnp.float32),
            pltpu.VMEM((2, 2, HIGH, BLOCK, LANES), jnp.float32),
            pltpu.VMEM((HIGH // 2, LANES, LANES), jnp.float32),
            pltpu.SemaphoreType.DMA((10,)),
        ],
        compiler_params=params,
        cost_estimate=cost(10**9),
        name="receiver_side",
    )(
        stay(layer_slowness),
        stay(layer_index.reshape(HIGH, LANES)),
        stay(field.reshape(2, BLOCK, NX)),
        stay(twiddles),
        stay(jnp.asarray(receiver_weights())),
        stay(wide),
        stay(jnp.asarray(window_twiddles())),
    )
    arrived = lax.all_to_all(chunks.reshape(groups, 16, LANES), "row", 0, 0, tiled=True, axis_index_groups=[row_order(groups)])
    parts, image = pl.pallas_call(
        second_kernel,
        out_shape=(keep(2, 2, PAIRS, 16, LANES), keep(total, BLOCK, HOFF)),
        in_specs=[vmem] * 6,
        out_specs=(vmem, vmem),
        scratch_shapes=[
            pltpu.VMEM((512, 256), jnp.float32),
            pltpu.VMEM((BLOCK, LANES), jnp.float32),
        ],
        compiler_params=params,
        cost_estimate=cost(10**9),
        name="shot_side",
    )(
        near(arrived.reshape(16 * groups, LANES)),
        near(corr),
        near(window),
        jnp.asarray(shot_weights()),
        jnp.asarray(shot_twiddles()),
        paired,
    )
    images = lax.all_to_all(image, "freq", 0, 0, tiled=True, axis_index_groups=[freq_order(total)])
    sunk = pl.pallas_call(
        third_kernel,
        out_shape=shape(2, BLOCK, NX),
        in_specs=[vmem, vmem],
        out_specs=vmem,
        compiler_params=params,
        cost_estimate=cost(10**8),
        name="shot_side_end",
    )(near(parts), near(corr))
    image = jnp.swapaxes(jnp.sum(images, axis=0), 0, 1)
    return jnp.swapaxes(sunk, 1, 2)[:, None], image


def solution(mesh):
    return jax.shard_map(
        on_device,
        mesh=mesh,
        in_specs=(P(None, "freq", "row", None), P(), P()),
        out_specs=(P(None, "freq", None, "row"), P(None, "row")),
        check_vma=False,
    )
```

```python
import math

import jax
import jax.numpy as jnp
import ml_dtypes
import numpy as np
from jax import lax
from jax.experimental import pallas as pl
from jax.experimental.pallas import tpu as pltpu
from jax.sharding import PartitionSpec as P

HOFF = 128
NX = 2048
NL = 16
BLOCK = 32
HIGH = 16
PAIRS = 32
LANES = 128

depth_step = 0.0125
grid_step = 0.0125
slow_slow = 1.0 / 1.5
slow_fast = 1.0 / 4.5
refs = (slow_slow, slow_fast)


def split16(table):
    high = table.astype(np.float32).astype(ml_dtypes.bfloat16)
    low = (table - high.astype(np.float64)).astype(np.float32).astype(ml_dtypes.bfloat16)
    return high, low


def real_form(matrix):
    return np.block([[matrix.real, matrix.imag], [-matrix.imag, matrix.real]])


def fourier(count):
    index = np.arange(count)
    return np.exp(-2j * math.pi * (index[:, None] * index[None, :] % count) / count)


def receiver_weights():
    forward = fourier(LANES)
    return np.stack([split16(forward.real), split16(-forward.imag)], axis=1)


def shot_weights():
    forward = fourier(64)
    same = np.eye(2)
    into = np.einsum("bsk,hg->bhsgk", forward.reshape(2, 32, 64), same).reshape(LANES, LANES)
    back = np.einsum("ks,hg->hkgs", forward.conj(), same).reshape(LANES, LANES)
    out = []
    for high, low in (split16(real_form(into)), split16(real_form(back))):
        out.append(np.concatenate([high, high, low]))
    return np.stack(out)


def twiddle_rows(count, position):
    angle = -2.0 * math.pi * np.arange(count)[:, None] * position[None, :] / NX
    return np.stack([np.cos(angle), np.sin(angle)]).astype(np.float32)


def shot_twiddles():
    lane = np.arange(LANES)
    into = twiddle_rows(PAIRS, lane // 64 * 32 + lane % 32)
    back = twiddle_rows(PAIRS, lane % 64)
    return np.stack([into, back])


def window_twiddles():
    lane = np.arange(LANES) % 64
    return np.stack([twiddle_rows(PAIRS, lane + 64 * m) for m in range(PAIRS)])


def window_start():
    return (lax.axis_index("row") * BLOCK + NX - HOFF // 2) & (NX - 1)


def omega_of(index, total):
    return 2.0 * math.pi * (5.0 + 30.0 * (index + 0.5) / total)


def propagators(total):
    index = np.arange(NX)
    knum = np.where(index < NX // 2, index, index - NX) * (2.0 * math.pi / (NX * grid_step))
    wide = np.zeros((total, 2, 2, HIGH, LANES), np.float32)
    paired = np.zeros((total, 2, 2, PAIRS, LANES), np.float32)
    for f in range(total):
        for j in range(2):
            quad = (omega_of(f, total) * refs[j]) ** 2 - knum**2
            mag = np.exp(-depth_step * np.sqrt(np.maximum(-quad, 0.0)))
            phase = -depth_step * np.sqrt(np.maximum(quad, 0.0))
            for c, values in enumerate((mag * np.cos(phase), mag * np.sin(phase))):
                wide[f, j, c] = values.reshape(LANES, HIGH).T
                paired[f, j, c] = np.tile(values.reshape(64, PAIRS).T, (1, 2))
    return wide, paired


def add(a, b):
    return a[0] + b[0], a[1] + b[1]


def sub(a, b):
    return a[0] - b[0], a[1] - b[1]


def mul(a, b):
    return a[0] * b[0] - a[1] * b[1], a[0] * b[1] + a[1] * b[0]


def mul_conj(a, b):
    return a[0] * b[0] + a[1] * b[1], a[1] * b[0] - a[0] * b[1]


def fft4(x, sign):
    t0, t1 = add(x[0], x[2]), sub(x[0], x[2])
    t2, t3 = add(x[1], x[3]), sub(x[1], x[3])
    up = (t1[0] - t3[1], t1[1] + t3[0])
    down = (t1[0] + t3[1], t1[1] - t3[0])
    if sign < 0:
        up, down = down, up
    return [add(t0, t2), up, sub(t0, t2), down]


def turn(x, step, count, sign):
    eighths = 8 * (step % count)
    if eighths == 0:
        return x
    if eighths == 2 * count:
        return (x[1], -x[0]) if sign < 0 else (-x[1], x[0])
    if eighths == count:
        root = math.sqrt(0.5)
        if sign < 0:
            return (x[0] + x[1]) * root, (x[1] - x[0]) * root
        return (x[0] - x[1]) * root, (x[1] + x[0]) * root
    angle = sign * 2.0 * math.pi * step / count
    return mul(x, (math.cos(angle), math.sin(angle)))


def fft(x, sign):
    count = len(x)
    if count == 1:
        return x
    if count == 2:
        return [add(x[0], x[1]), sub(x[0], x[1])]
    if count == 4:
        return fft4(x, sign)
    first = 4 if count > 8 else 2
    second = count // first
    parts = [fft([x[second * m + n] for m in range(first)], sign) for n in range(second)]
    out = [None] * count
    for k in range(first):
        column = fft([turn(parts[n][k], n * k, count, sign) for n in range(second)], sign)
        for m in range(second):
            out[k + first * m] = column[m]
    return out


def halves(x):
    high = x.astype(jnp.bfloat16)
    return high, (x - high.astype(jnp.float32)).astype(jnp.bfloat16)


def dot3(x, w):
    high, low = halves(x)
    return jnp.dot(jnp.concatenate([high, low, high], axis=1), w, preferred_element_type=jnp.float32)


def row(ref, i):
    return ref[pl.ds(i, 1), :]


def scatter_up(x, tw, out_ref, rows, at):
    for k, tile in enumerate(fft(x, -1)):
        turned = mul(tile, (row(tw.at[0], k), row(tw.at[1], k)))
        for c in range(2):
            out_ref[rows * k + at : rows * k + at + 8, LANES * c : LANES * (c + 1)] = turned[c]


def middle(in_ref, rows, w_ref, e_ref, tw, out_ref):
    count = in_ref.shape[0] // rows
    spec = dot3(in_ref[...], w_ref[0])
    for j in range(2):
        moved = []
        for k in range(count):
            part = spec[k * rows : (k + 1) * rows]
            e = (row(e_ref.at[0, j, 0], k), row(e_ref.at[0, j, 1], k))
            moved.append(jnp.concatenate(mul((part[:, :LANES], part[:, LANES:]), e), axis=1))
        back = dot3(jnp.concatenate(moved, axis=0), w_ref[1])
        tiles = []
        for k in range(count):
            part = back[k * rows : (k + 1) * rows]
            tiles.append((part[:, :LANES], part[:, LANES:]))
            turned = mul_conj(tiles[k], (row(tw.at[0], k), row(tw.at[1], k)))
            for c in range(2):
                out_ref[j, c, k] = turned[c]
        yield j, tiles


def window_tiles(tiles, tw):
    sums = [None] * 3
    for k in range(8):
        part = [mul_conj(tiles[k + n], (row(tw.at[0], k + n), row(tw.at[1], k + n))) for n in range(0, 32, 8)]
        even = add(part[0], part[2]), add(part[1], part[3])
        odd = sub(part[0], part[2]), sub(part[1], part[3])
        odd = (odd[0][0] - odd[1][1], odd[0][1] + odd[1][0])
        terms = (add(*even), turn(odd, k, 32, 1), turn(sub(*even), k, 16, 1))
        sums = [t if p is None else add(p, t) for p, t in zip(sums, terms)]
    return sums


def gather_up(tiles_of, corr_of):
    result = None
    for j in range(2):
        terms = [mul(v, corr_of(j, a)) for a, v in enumerate(fft(tiles_of(j), 1))]
        result = terms if result is None else [add(r, t) for r, t in zip(result, terms)]
    return result


def corrections(index, slow_ref, omega):
    slowness = jnp.zeros(index.shape, jnp.float32)
    for layer in range(NL):
        slowness = jnp.where(index == layer, slow_ref[layer], slowness)
    upper = (slow_slow - slowness) / (slow_slow - slow_fast)
    weights = (1.0 - upper, upper)
    out = []
    for j in range(2):
        angle = -omega * depth_step * (slowness - refs[j])
        scale = weights[j] * (1.0 / NX)
        out.append((scale * jnp.cos(angle), scale * jnp.sin(angle)))
    return out


def exchange(x, y, mask, width):
    return (
        jnp.where(mask, x, pltpu.roll(y, width, 1)),
        jnp.where(mask, pltpu.roll(x, LANES - width, 1), y),
    )


def place(block):
    return 19 * block % 64


def row_order(groups):
    order = [0] * groups
    for block in range(groups):
        order[place(block)] = block
    return order


def freq_order(total):
    return [3 * i % total for i in range(total)]


def lanes_of(rows):
    return lax.broadcasted_iota(jnp.int32, (rows, LANES), 1)


def first_kernel(
    total, slow_hbm, index_hbm, field_hbm, tw_hbm, w_hbm, e_hbm, window_hbm, out_ref, corr_ref, window_ref,
    slow_ref, index_ref, field_ref, tw_ref, wave_ref, e_ref, own_ref, w_ref, mid_ref, back_ref, sunk, sems,
):
    freq = lax.axis_index("freq")
    pairs = [
        (slow_hbm, slow_ref),
        (index_hbm, index_ref),
        (tw_hbm, tw_ref),
        (w_hbm, wave_ref),
        (e_hbm.at[pl.ds(freq, 1)], e_ref),
    ]
    for at in range(0, BLOCK, 8):
        pairs.append((field_hbm.at[:, pl.ds(at, 8)], field_ref.at[:, pl.ds(at, 8)]))
    pairs.append((window_hbm.at[window_start() >> 6], window_ref))
    copies = [pltpu.make_async_copy(s, d, sems.at[i]) for i, (s, d) in enumerate(pairs)]
    for copy in copies:
        copy.start()
    copies[0].wait()
    copies[1].wait()
    omega = 2.0 * math.pi * (5.0 + 30.0 * (freq.astype(jnp.float32) + 0.5) / total)
    left = lanes_of(HIGH) < 64
    for j, values in enumerate(corrections(index_ref[...], slow_ref, omega)):
        for c in range(2):
            own_ref[j, c] = values[c]
            other = pltpu.roll(values[c], 64, 1)
            corr_ref[j, c, 0] = jnp.where(left, values[c], other)
            corr_ref[j, c, 1] = jnp.where(left, other, values[c])
    copies[2].wait()
    copies[3].wait()
    copies[4].wait()
    for part, level in enumerate((0, 0, 1)):
        for way, sign in enumerate((1, -1)):
            cos, sin = wave_ref[level, 0], wave_ref[level, 1] * sign
            for at, blocks in enumerate(((cos, -sin), (sin, cos))):
                for c in range(2):
                    base = 256 * part + LANES * at
                    w_ref[way, base : base + LANES, LANES * c : LANES * (c + 1)] = blocks[c]
    for i, at in enumerate(range(0, BLOCK, 8)):
        copies[5 + i].wait()
        x = [
            tuple(field_ref[c, at : at + 8, LANES * a : LANES * (a + 1)] for c in range(2))
            for a in range(HIGH)
        ]
        scatter_up(x, tw_ref, mid_ref, BLOCK, at)
    for _ in middle(mid_ref, BLOCK, w_ref, e_ref, tw_ref, back_ref):
        pass
    copies[9].wait()
    for at in range(0, BLOCK, 8):
        u = gather_up(
            lambda j: [tuple(back_ref[j, c, k, at : at + 8, :] for c in range(2)) for k in range(HIGH)],
            lambda j, a: (row(own_ref.at[j, 0], a), row(own_ref.at[j, 1], a)),
        )
        for a in range(HIGH):
            for c in range(2):
                base = c * 64 + (a % 2) * 32 + at
                sunk[a // 2, base : base + 8, :] = u[a][c]
    even = (lanes_of(16) & 63) < 32
    for p in range(HIGH // 2):
        turned = sunk[p].T
        for q in range(4):
            first, second = exchange(turned[32 * q : 32 * q + 16], turned[32 * q + 16 : 32 * q + 32], even, 32)
            for block, chunk in ((8 * p + q, first), (8 * p + 4 + q, second)):
                out_ref[16 * place(block) : 16 * place(block) + 16, :] = chunk


def second_kernel(in_ref, corr_ref, window_ref, w_ref, tw_ref, e_all, parts_ref, images_ref, mid_ref, image_ref):
    e_ref = e_all.at[pl.ds(lax.axis_index("freq"), 1)]
    left = lanes_of(8) < 64
    for at in (0, 8):
        x = []
        for m in range(PAIRS):
            first, second = (
                in_ref[16 * place(2 * m + i) + at : 16 * place(2 * m + i) + at + 8, :] for i in range(2)
            )
            x.append(exchange(first, second, left, 64))
        scatter_up(x, tw_ref.at[0], mid_ref, 16, at)
    start = window_start()
    offset = start & 63
    strips = [None] * 3
    for j, tiles in middle(mid_ref, 16, w_ref, e_ref, tw_ref.at[1], parts_ref):
        for i, here in enumerate(window_tiles(tiles, window_ref)):
            m = ((start >> 6) + i) & (PAIRS - 1)
            c = (row(corr_ref.at[j, 0, m & 1], m >> 1), row(corr_ref.at[j, 1, m & 1], m >> 1))
            term = here[0] * c[0] - here[1] * c[1]
            strips[i] = term if j == 0 else strips[i] + term
    left = lanes_of(16) < 64
    bands = zip(exchange(strips[0], strips[1], left, 64), (strips[2], pltpu.roll(strips[2], 64, 1)))
    line = lax.broadcasted_iota(jnp.int32, (8, LANES), 0)
    lane = lanes_of(8)
    for h, (near, far) in enumerate(bands):
        for at in (0, 8):
            image = None
            for i in range(8):
                width = offset + 16 * h + at + i
                back = (LANES - width) & (LANES - 1)
                moved = jnp.where(
                    lane < LANES - width,
                    pltpu.roll(near[at : at + 8], back, 1),
                    pltpu.roll(far[at : at + 8], back, 1),
                )
                image = moved if image is None else jnp.where(line == i, moved, image)
            image_ref[16 * h + at : 16 * h + at + 8, :] = image
    for f in range(images_ref.shape[0]):
        images_ref[f] = image_ref[...]


def third_kernel(parts_ref, corr_ref, out_ref):
    left = lanes_of(8) < 64
    for at in (0, 8):
        u = gather_up(
            lambda j: [tuple(parts_ref[j, c, k, at : at + 8, :] for c in range(2)) for k in range(PAIRS)],
            lambda j, m: tuple(row(corr_ref.at[j, c, m % 2], m // 2) for c in range(2)),
        )
        for a in range(HIGH):
            for c in range(2):
                for h, tile in enumerate(exchange(u[2 * a][c], u[2 * a + 1][c], left, 64)):
                    out_ref[c, 16 * h + at : 16 * h + at + 8, LANES * a : LANES * (a + 1)] = tile


def on_device(field, layer_index, layer_slowness):
    total = lax.axis_size("freq")
    groups = lax.axis_size("row")
    wide, paired = (jnp.asarray(table) for table in propagators(total))
    twiddles = jnp.asarray(twiddle_rows(HIGH, np.arange(LANES)))
    shape = lambda *dims: jax.ShapeDtypeStruct(dims, jnp.float32)
    keep = lambda *dims: pltpu.VMEM(dims, jnp.float32)
    vmem = pl.BlockSpec(memory_space=pltpu.VMEM)
    hbm = pl.BlockSpec(memory_space=pltpu.HBM)
    stay = lambda x: pltpu.with_memory_space_constraint(x, pltpu.HBM)
    near = lambda x: pltpu.with_memory_space_constraint(x, pltpu.VMEM)
    params = pltpu.CompilerParams(vmem_limit_bytes=32 * 2**20)
    cost = lambda n: pl.CostEstimate(flops=n, bytes_accessed=2**20, transcendentals=0)
    chunks, corr, window = pl.pallas_call(
        lambda *a: first_kernel(total, *a),
        out_shape=(keep(16 * groups, LANES), keep(2, 2, 2, HIGH, LANES), keep(2, PAIRS, LANES)),
        in_specs=[hbm] * 7,
        out_specs=(vmem, vmem, vmem),
        scratch_shapes=[
            pltpu.SMEM((NL,), jnp.float32),
            pltpu.VMEM((HIGH, LANES), jnp.int32),
            pltpu.VMEM((2, BLOCK, NX), jnp.float32),
            pltpu.VMEM((2, HIGH, LANES), jnp.float32),
            pltpu.VMEM((2, 2, LANES, LANES), jnp.bfloat16),
            pltpu.VMEM((1, 2, 2, HIGH, LANES), jnp.float32),
            pltpu.VMEM((2, 2, HIGH, LANES), jnp.float32),
            pltpu.VMEM((2, 768, 256), jnp.bfloat16),
            pltpu.VMEM((512, 256), jnp.float32),
            pltpu.VMEM((2, 2, HIGH, BLOCK, LANES), jnp.float32),
            pltpu.VMEM((HIGH // 2, LANES, LANES), jnp.float32),
            pltpu.SemaphoreType.DMA((10,)),
        ],
        compiler_params=params,
        cost_estimate=cost(10**9),
        name="receiver_side",
    )(
        stay(layer_slowness),
        stay(layer_index.reshape(HIGH, LANES)),
        stay(field.reshape(2, BLOCK, NX)),
        stay(twiddles),
        stay(jnp.asarray(receiver_weights())),
        stay(wide),
        stay(jnp.asarray(window_twiddles())),
    )
    arrived = lax.all_to_all(chunks.reshape(groups, 16, LANES), "row", 0, 0, tiled=True, axis_index_groups=[row_order(groups)])
    parts, image = pl.pallas_call(
        second_kernel,
        out_shape=(keep(2, 2, PAIRS, 16, LANES), keep(total, BLOCK, HOFF)),
        in_specs=[vmem] * 6,
        out_specs=(vmem, vmem),
        scratch_shapes=[
            pltpu.VMEM((512, 256), jnp.float32),
            pltpu.VMEM((BLOCK, LANES), jnp.float32),
        ],
        compiler_params=params,
        cost_estimate=cost(10**9),
        name="shot_side",
    )(
        near(arrived.reshape(16 * groups, LANES)),
        near(corr),
        near(window),
        jnp.asarray(shot_weights()),
        jnp.asarray(shot_twiddles()),
        paired,
    )
    images = lax.all_to_all(image, "freq", 0, 0, tiled=True, axis_index_groups=[freq_order(total)])
    sunk = pl.pallas_call(
        third_kernel,
        out_shape=shape(2, BLOCK, NX),
        in_specs=[vmem, vmem],
        out_specs=vmem,
        compiler_params=params,
        cost_estimate=cost(10**8),
        name="shot_side_end",
    )(near(parts), near(corr))
    image = jnp.swapaxes(jnp.sum(images, axis=0), 0, 1)
    return jnp.swapaxes(sunk, 1, 2)[:, None], image


def solution(mesh):
    return jax.shard_map(
        on_device,
        mesh=mesh,
        in_specs=(P(None, "freq", "row", None), P(), P()),
        out_specs=(P(None, "freq", None, "row"), P(None, "row")),
        check_vma=False,
    )
```
